256 devices in a mesh: grp: 32 (over x, y, core), sub: 8 (over z).
Axes of the slice: x: 4, y: 4, z: 8, core: 2. Of those that a mesh axis runs over, the one named last changes fastest.
Arguments:
- q_local: bfloat16 [32768, 1024], P(('grp', 'sub')), may hold values from -6 to 6
- k_local: bfloat16 [32768, 1024], P(('grp', 'sub')), may hold values from -6 to 6
- v_local: bfloat16 [32768, 1024], P(('grp', 'sub')), may hold values from -6 to 6
- q_short: bfloat16 [4096, 1024], P(('grp', 'sub')), may hold values from -6 to 6
- k_short: bfloat16 [4096, 1024], P(('grp', 'sub')), may hold values from -6 to 6
- v_short: bfloat16 [4096, 1024], P(('grp', 'sub')), may hold values from -6 to 6
- grad_out: bfloat16 [32768, 1024], P(('grp', 'sub')), may hold values from -6 to 6
Outputs:
- local_out: bfloat16 [32768, 1024], P(('grp', 'sub'))
- local_dq: bfloat16 [32768, 1024], P(('grp', 'sub'))
- local_dk: bfloat16 [32768, 1024], P(('grp', 'sub'))
- local_dv: bfloat16 [32768, 1024], P(('grp', 'sub'))
- short_out: bfloat16 [4096, 1024], P('grp', 'sub')
- short_dq: bfloat16 [4096, 1024], P('grp', 'sub')
- short_dk: bfloat16 [4096, 1024], P('grp', 'sub')
- short_dv: bfloat16 [4096, 1024], P('grp', 'sub')
The draws below stay inside these ranges and needn't reach their ends.
All inputs are finite; a program needn't handle non-finite values.
Results may differ from the reference program's by a relative error of at most 0.0318.
Values may be sent and summed in bfloat16 or wider, within the bound.
No kernel may reach another device: no remote copies, remote signals or barrier semaphores. Data moves between devices by JAX's collectives and lax.ppermute only.
A program may use at most 64 MiB of HBM per device.

```python
import math
import jax
import jax.numpy as jnp
from jax import lax

D = 1024
H = 16
HD = 64
WINDOW = 128
POOL = 8
TOK_DEV = 128
TOKENS = 32768
SHORT = 4096
N_GRP = 32


def aligned_pair(key, num_rows, feat_width, head_size, strong):
    subkeys = jax.random.split(key, 7)
    position = jnp.arange(num_rows)
    queries = jax.random.truncated_normal(subkeys[0], -3.0, 3.0, (num_rows, feat_width), jnp.float32)
    targets = jax.random.truncated_normal(subkeys[1], -3.0, 3.0, (num_rows, feat_width), jnp.float32)
    chosen = jax.random.bernoulli(subkeys[4], 1.0 / 64.0, (num_rows,)) & (position % 2 == 0) & (position >= 2) & (strong > 0.0)
    level_table = jnp.array([4.0, 4.8, 5.5], jnp.float32)
    levels = level_table[jax.random.randint(subkeys[5], (num_rows,), 0, 3)]
    sign_table = jnp.where(jax.random.bernoulli(subkeys[6], 0.5, (num_rows, feat_width)), 1.0, -1.0)
    peak_rows = levels[:, None] * sign_table
    queries = jnp.where(chosen[:, None], peak_rows, queries)
    targets = jnp.where(chosen[:, None], peak_rows, targets)
    near_factor = 1.0 - 2.0 / math.sqrt(head_size) / (levels * levels)
    after_chosen = jnp.concatenate([chosen[1:], jnp.zeros((1,), bool)])
    shifted = jnp.concatenate([peak_rows[1:] * near_factor[1:, None], jnp.zeros((1, feat_width), jnp.float32)], axis=0)
    targets = jnp.where(after_chosen[:, None], shifted, targets)
    return (queries, targets)


def draw_q_local(key, part):
    strong = 0.0
    return aligned_pair(jax.random.fold_in(key, 7), TOKENS, D, HD, strong)[0].astype(jnp.bfloat16)


def draw_k_local(key, part):
    strong = 0.0
    return aligned_pair(jax.random.fold_in(key, 7), TOKENS, D, HD, strong)[1].astype(jnp.bfloat16)


def draw_q_short(key, part):
    strong = 0.0
    return aligned_pair(jax.random.fold_in(key, 11), SHORT, D, HD, strong)[0].astype(jnp.bfloat16)


def draw_k_short(key, part):
    strong = 0.0
    return aligned_pair(jax.random.fold_in(key, 11), SHORT, D, HD, strong)[1].astype(jnp.bfloat16)


def steps_of(own_key, dims, cuts, low, high):
    def one(dim, shards_of):
        heights = jax.random.uniform(jax.random.fold_in(jax.random.fold_in(own_key, 6), dim), (shards_of,), jnp.float32, low / len(cuts), high / len(cuts))
        return jnp.repeat(jnp.exp(heights), dims[dim] // shards_of).reshape((-1,) + (1,) * (len(dims) - dim - 1))

    factor_of = one(*cuts[0])
    for cut in cuts[1:]:
        factor_of = factor_of * one(*cut)
    return factor_of


def scatter_about(own_key, extent, scale, reach, cuts=(), kind=jnp.bfloat16):
    values = jax.random.normal(own_key, extent, jnp.float32) * scale
    if len(cuts) > 0:
        values = steps_of(own_key, extent, cuts, -0.22, 0.18) * values
    return jnp.clip(values, min=-reach, max=reach).astype(kind)


def setup_inputs(seed: int = 0) -> dict:
    arg_keys = jax.random.split(jax.random.key(seed), 8)
    return {
        "q_local": draw_q_local(jax.random.fold_in(arg_keys[7], 71), 0),
        "k_local": draw_k_local(jax.random.fold_in(arg_keys[7], 71), 0),
        "v_local": scatter_about(arg_keys[2], (TOKENS, D), 1.0, 6.0, ((0, 256),)),
        "q_short": draw_q_short(jax.random.fold_in(arg_keys[7], 71), 0),
        "k_short": draw_k_short(jax.random.fold_in(arg_keys[7], 71), 0),
        "v_short": scatter_about(arg_keys[5], (SHORT, D), 1.0, 6.0, ((0, 256),)),
        "grad_out": scatter_about(arg_keys[6], (TOKENS, D), 1.0, 6.0, ((0, 256),)),
    }


def attend(queries, key_rows, values, cotangent, key_mask, score_scale):
    q_full = queries.astype(jnp.float32)
    k_full = key_rows.astype(jnp.float32)
    v_full = values.astype(jnp.float32)
    g_full = cotangent.astype(jnp.float32)
    scores = jnp.einsum('ihd,jhd->hij', q_full, k_full) * score_scale
    scores = jnp.where(key_mask[None], scores, -jnp.inf)
    row_max = lax.optimization_barrier(jnp.max(scores, axis=-1))
    log_total = row_max + jnp.log(lax.optimization_barrier(jnp.sum(jnp.exp(scores - row_max[..., None]), axis=-1)))
    weights = jnp.exp(scores - log_total[..., None])
    weights_bf = lax.optimization_barrier(weights.astype(jnp.bfloat16)).astype(jnp.float32)
    output = jnp.einsum('hij,jhd->ihd', weights_bf, v_full).astype(jnp.bfloat16)
    out_full = lax.optimization_barrier(output).astype(jnp.float32)
    row_dots = jnp.einsum('ihd,ihd->hi', g_full, out_full)
    dprob = jnp.einsum('ihd,jhd->hij', g_full, v_full)
    dscore = weights * (dprob - row_dots[..., None])
    dscore = lax.optimization_barrier(dscore.astype(jnp.bfloat16)).astype(jnp.float32)
    grad_q = (jnp.einsum('hij,jhd->ihd', dscore, k_full) * score_scale).astype(jnp.bfloat16)
    grad_k = jnp.einsum('hij,ihd->jhd', dscore, q_full) * score_scale
    grad_v = jnp.einsum('hij,ihd->jhd', weights_bf, g_full)
    return (output, grad_q, grad_k, grad_v)

def local_layer(q_local, k_local, v_local, grad_out, score_scale):
    block = TOK_DEV
    num_blocks = TOKENS // block
    k_padded = jnp.concatenate([jnp.zeros((block, D), k_local.dtype), k_local], axis=0)
    v_padded = jnp.concatenate([jnp.zeros((block, D), v_local.dtype), v_local], axis=0)

    def block_step(running, index):
        first_row = index * block
        queries = lax.dynamic_slice_in_dim(q_local, first_row, block, 0).reshape(block, H, HD)
        cotangent = lax.dynamic_slice_in_dim(grad_out, first_row, block, 0).reshape(block, H, HD)
        key_rows = lax.dynamic_slice_in_dim(k_padded, first_row, 2 * block, 0).reshape(2 * block, H, HD)
        value_rows = lax.dynamic_slice_in_dim(v_padded, first_row, 2 * block, 0).reshape(2 * block, H, HD)
        query_pos = first_row + jnp.arange(block, dtype=jnp.int32)
        key_pos = first_row - block + jnp.arange(2 * block, dtype=jnp.int32)
        key_mask = (key_pos[None, :] <= query_pos[:, None]) & (key_pos[None, :] > query_pos[:, None] - WINDOW) & (key_pos[None, :] >= 0)
        output, grad_q, grad_k, grad_v = attend(queries, key_rows, value_rows, cotangent, key_mask, score_scale)
        grad_k = grad_k.reshape(2 * block, D)
        grad_v = grad_v.reshape(2 * block, D)
        own_k = (grad_k[block:] + running[0]).astype(jnp.bfloat16)
        own_v = (grad_v[block:] + running[1]).astype(jnp.bfloat16)
        return ((grad_k[:block], grad_v[:block]), (output.reshape(block, D), grad_q.reshape(block, D), own_k, own_v))
    start_terms = (jnp.zeros((block, D), jnp.float32), jnp.zeros((block, D), jnp.float32))
    unused, stacked = lax.scan(block_step, start_terms, jnp.arange(num_blocks, dtype=jnp.int32), reverse=True)
    return tuple((piece.reshape(TOKENS, D) for piece in stacked))

def short_layer(q_short, k_short, v_short, grad_out, score_scale):
    group_rows = SHORT // N_GRP
    pooled = lax.optimization_barrier(jnp.sum(grad_out.reshape(SHORT, POOL, D), axis=1, dtype=jnp.float32)).astype(jnp.bfloat16)
    key_rows = k_short.reshape(SHORT, H, HD)
    value_rows = v_short.reshape(SHORT, H, HD)
    key_pos = jnp.arange(SHORT, dtype=jnp.int32)

    def block_step(running, index):
        first_row = index * group_rows
        queries = lax.dynamic_slice_in_dim(q_short, first_row, group_rows, 0).reshape(group_rows, H, HD)
        cotangent = lax.dynamic_slice_in_dim(pooled, first_row, group_rows, 0).reshape(group_rows, H, HD)
        query_pos = first_row + jnp.arange(group_rows, dtype=jnp.int32)
        key_mask = key_pos[None, :] <= query_pos[:, None]
        output, grad_q, grad_k, grad_v = attend(queries, key_rows, value_rows, cotangent, key_mask, score_scale)
        return ((running[0] + grad_k, running[1] + grad_v), (output.reshape(group_rows, D), grad_q.reshape(group_rows, D)))
    start_terms = (jnp.zeros((SHORT, H, HD), jnp.float32), jnp.zeros((SHORT, H, HD), jnp.float32))
    sums, stacked = lax.scan(block_step, start_terms, jnp.arange(N_GRP, dtype=jnp.int32))
    short_out = stacked[0].reshape(SHORT, D)
    short_dq = stacked[1].reshape(SHORT, D)
    short_dk = sums[0].reshape(SHORT, D).astype(jnp.bfloat16)
    short_dv = sums[1].reshape(SHORT, D).astype(jnp.bfloat16)
    return (short_out, short_dq, short_dk, short_dv)

def reference(q_local, k_local, v_local, q_short, k_short, v_short, grad_out):
    score_scale = 1.0 / math.sqrt(HD)
    local_out, local_dq, local_dk, local_dv = local_layer(q_local, k_local, v_local, grad_out, score_scale)
    short_out, short_dq, short_dk, short_dv = short_layer(q_short, k_short, v_short, grad_out, score_scale)
    return (local_out, local_dq, local_dk, local_dv, short_out, short_dq, short_dk, short_dv)
```

```python
import math

import jax
import jax.numpy as jnp
from jax import lax
from jax.experimental import pallas as pl
from jax.experimental.pallas import tpu as pltpu
from jax.sharding import Mesh
from jax.sharding import PartitionSpec as P

HD = 64
WINDOW = 128
POOL = 8
LANES = 128
NEG = float("-inf")


def dot_t(a, b):
    return lax.dot_general(a, b, (((1,), (1,)), ((), ())), preferred_element_type=jnp.float32)


def dot_n(a, b):
    return lax.dot_general(a, b, (((1,), (0,)), ((), ())), preferred_element_type=jnp.float32)


def t_dot(a, b):
    return lax.dot_general(a, b, (((0,), (0,)), ((), ())), preferred_element_type=jnp.float32)


def local_kernel(first_ref, q_ref, k_ref, v_ref, g_ref, pk_ref, pv_ref,
                 out_ref, dq_ref, dk_ref, dv_ref, bk_ref, bv_ref):
    rows, width = q_ref.shape
    scale = 1.0 / math.sqrt(HD)
    lane = lax.broadcasted_iota(jnp.int32, (rows, LANES), 1)
    low = lane < HD
    row2 = lax.broadcasted_iota(jnp.int32, (2 * rows, rows), 0) & (rows - 1)
    col2 = lax.broadcasted_iota(jnp.int32, (2 * rows, rows), 1)
    from_prev = col2 > row2
    dead = from_prev & (first_ref[0] == 0)
    zero_b = jnp.zeros((rows, LANES), jnp.bfloat16)
    zero_f = jnp.zeros((2 * rows, rows), jnp.bfloat16)
    for pair in range(width // LANES):
        cols = slice(pair * LANES, (pair + 1) * LANES)
        q, g = q_ref[:, cols], g_ref[:, cols]
        q2 = jnp.concatenate([jnp.where(low, q, zero_b), jnp.where(low, zero_b, q)], axis=0)
        g2 = jnp.concatenate([jnp.where(low, g, zero_b), jnp.where(low, zero_b, g)], axis=0)
        kc = jnp.concatenate([pk_ref[:, cols], k_ref[:, cols]], axis=0)
        vc = jnp.concatenate([pv_ref[:, cols], v_ref[:, cols]], axis=0)
        s_all = dot_t(q2, kc)
        s = jnp.where(from_prev, s_all[:, :rows], s_all[:, rows:]) * scale
        s = jnp.where(dead, NEG, s)
        p = jnp.exp(s - jnp.max(s, axis=1, keepdims=True))
        p = p * (1.0 / jnp.sum(p, axis=1, keepdims=True))
        pb = p.astype(jnp.bfloat16)
        pc = jnp.concatenate(
            [jnp.where(from_prev, pb, zero_f), jnp.where(from_prev, zero_f, pb)], axis=1)
        o2 = dot_n(pc, vc).astype(jnp.bfloat16)
        out_ref[:, cols] = jnp.where(low, o2[:rows], o2[rows:])
        dots = jnp.sum(g2.astype(jnp.float32) * o2.astype(jnp.float32), axis=1, keepdims=True)
        dp_all = dot_t(g2, vc)
        dp = jnp.where(from_prev, dp_all[:, :rows], dp_all[:, rows:])
        ds = (p * (dp - dots)).astype(jnp.bfloat16)
        dc = jnp.concatenate(
            [jnp.where(from_prev, ds, zero_f), jnp.where(from_prev, zero_f, ds)], axis=1)
        dq2 = dot_n(dc, kc) * scale
        dq_ref[:, cols] = jnp.where(low, dq2[:rows], dq2[rows:]).astype(jnp.bfloat16)
        dkc = t_dot(dc, q2) * scale
        dvc = t_dot(pc, g2)
        bk_ref[:, cols] = dkc[:rows].astype(jnp.bfloat16)
        bv_ref[:, cols] = dvc[:rows].astype(jnp.bfloat16)
        dk_ref[:, cols] = dkc[rows:]
        dv_ref[:, cols] = dvc[rows:]


def local_call(first, q, k, v, g, pk, pv):
    rows, width = q.shape
    wide = jax.ShapeDtypeStruct((rows, width), jnp.float32)
    half = jax.ShapeDtypeStruct((rows, width), jnp.bfloat16)
    vm = pl.BlockSpec(memory_space=pltpu.VMEM)
    return pl.pallas_call(
        local_kernel,
        out_shape=(half, half, wide, wide, half, half),
        in_specs=[pl.BlockSpec(memory_space=pltpu.SMEM)] + [vm] * 6,
        out_specs=(vm,) * 6,
        compiler_params=pltpu.CompilerParams(vmem_limit_bytes=32 * 1024 * 1024),
        cost_estimate=pl.CostEstimate(
            flops=12 * rows * 256 * width * 2, bytes_accessed=12 * rows * width * 2,
            transcendentals=rows * rows * 16),
        name="local_layer",
    )(first, q, k, v, g, pk, pv)


def pack_kernel(q_ref, k_ref, v_ref, g_ref, packed_ref):
    small = q_ref.shape[0]
    low = lax.broadcasted_iota(jnp.int32, (small, LANES), 1) < HD

    def halves(a, b):
        swap_a = pltpu.roll(a, HD, 1)
        swap_b = pltpu.roll(b, HD, 1)
        return jnp.where(low, a, swap_b), jnp.where(low, swap_a, b)

    pairs = q_ref.shape[1] // LANES
    for pair in range(pairs):
        cols = slice(pair * LANES, (pair + 1) * LANES)
        grads = g_ref[:, cols].astype(jnp.float32).reshape(small, POOL, LANES)
        pooled = jnp.sum(grads, axis=1).astype(jnp.bfloat16).astype(jnp.float32)
        quarter = [r[:, cols].astype(jnp.float32) for r in (q_ref, k_ref, v_ref)]
        qg = halves(quarter[0], pooled)
        kv = halves(quarter[1], quarter[2])
        for core in range(2):
            packed_ref[core * pairs + pair, :, :LANES] = qg[core].astype(jnp.bfloat16)
            packed_ref[core * pairs + pair, :, LANES:] = kv[core].astype(jnp.bfloat16)


def pack_call(q, k, v, g):
    small, width = q.shape
    vm = pl.BlockSpec(memory_space=pltpu.VMEM)
    return pl.pallas_call(
        pack_kernel,
        out_shape=jax.ShapeDtypeStruct((width // HD, small, 4 * HD), jnp.bfloat16),
        in_specs=[vm] * 4,
        out_specs=vm,
        name="pack_heads",
    )(q, k, v, g)


def spread_kernel(mine_ref, many_ref, late_ref, kv_ref, sem):
    kv_ref[...] = mine_ref[:, LANES:]
    copies = [pltpu.make_async_copy(kv_ref, many_ref.at[i], sem.at[i])
              for i in range(many_ref.shape[0])]
    for copy in copies:
        copy.start()
    half = mine_ref.shape[0] // 2
    late_ref[...] = mine_ref[half:, :LANES]
    for copy in copies:
        copy.wait()


def spread_call(mine, chips):
    rows = mine.shape[0]
    vm = pl.BlockSpec(memory_space=pltpu.VMEM)
    return pl.pallas_call(
        spread_kernel,
        out_shape=(jax.ShapeDtypeStruct((chips, rows, LANES), jnp.bfloat16),
                   jax.ShapeDtypeStruct((rows // 2, LANES), jnp.bfloat16)),
        in_specs=[vm],
        out_specs=(pl.BlockSpec(memory_space=pl.ANY), vm),
        scratch_shapes=[pltpu.VMEM((rows, LANES), jnp.bfloat16), pltpu.SemaphoreType.DMA((chips,))],
        name="spread_keys",
    )(mine)


def short_kernel(chip_ref, mine_ref, late_ref, kv_ref, od_a_ref, od_b_ref, dkv_ref,
                 lhs_ref, lhs_t_ref, s_ref, dp_ref, top_ref, sum_ref, dot_ref, od_ref, acc_ref):
    scale = 1.0 / math.sqrt(HD)
    chip = chip_ref[0]
    blocks, _, kb = acc_ref.shape
    half = late_ref.shape[0]
    low = lax.broadcasted_iota(jnp.int32, (half, LANES), 1) < HD
    zero_b = jnp.zeros((half, LANES), jnp.bfloat16)
    for which, qg in enumerate((mine_ref[:half, :LANES], late_ref[...])):
        qz = jnp.where(low, (qg.astype(jnp.float32) * scale).astype(jnp.bfloat16), zero_b)
        gz = jnp.where(low, zero_b, qg)
        lhs = jnp.concatenate([qz, gz], axis=0)
        lhs_ref[which] = lhs
        lhs_t_ref[which] = lhs.T
    top_ref[...] = jnp.full_like(top_ref, NEG)
    sum_ref[...] = jnp.zeros_like(sum_ref)
    dot_ref[...] = jnp.zeros_like(dot_ref)
    od_ref[...] = jnp.zeros_like(od_ref)
    acc_ref[...] = jnp.zeros_like(acc_ref)
    ahead = (lax.broadcasted_iota(jnp.int32, (half, kb), 1)
             - lax.broadcasted_iota(jnp.int32, (half, kb), 0))
    steps = blocks + 1

    def place(t):
        second = t > chip
        which = jnp.where(second, 1, 0)
        block = jnp.where(second, t - chip - 1, t)
        first = jnp.where(second, (blocks - 1 - chip) * kb + half, chip * kb)
        return which, block, first - block * kb

    def keys(block):
        return kv_ref[pl.ds(pl.multiple_of(block * kb, kb), kb), :]

    for t in range(steps):
        which, block, reach = place(t)
        both = dot_t(lhs_ref[which], keys(block))
        s = jnp.where(ahead <= reach, both[:half], NEG)
        s_ref[t] = s
        dp_ref[t] = both[half:]
        top_ref[which] = jnp.maximum(top_ref[which], jnp.maximum(s[:, :LANES], s[:, LANES:]))
    for which in range(2):
        top = jnp.max(top_ref[which], axis=1, keepdims=True)
        top_ref[which] = jnp.broadcast_to(top, (half, LANES))
    for t in range(steps):
        which, _, _ = place(t)
        top = top_ref[which]
        e = jnp.exp(s_ref[t] - jnp.concatenate([top, top], axis=1))
        s_ref[t] = e
        ed = e * dp_ref[t]
        sum_ref[which] = sum_ref[which] + (e[:, :LANES] + e[:, LANES:])
        dot_ref[which] = dot_ref[which] + (ed[:, :LANES] + ed[:, LANES:])
    for which in range(2):
        inv = 1.0 / jnp.sum(sum_ref[which], axis=1, keepdims=True)
        dots = jnp.sum(dot_ref[which], axis=1, keepdims=True) * inv
        sum_ref[which] = jnp.broadcast_to(inv, (half, LANES))
        dot_ref[which] = jnp.broadcast_to(dots, (half, LANES))
    for t in range(steps):
        which, block, _ = place(t)
        inv, dots = sum_ref[which], dot_ref[which]
        p = s_ref[t] * jnp.concatenate([inv, inv], axis=1)
        ds = p * (dp_ref[t] - jnp.concatenate([dots, dots], axis=1))
        dsp = jnp.concatenate([ds.astype(jnp.bfloat16), p.astype(jnp.bfloat16)], axis=0)
        oq = dot_n(dsp, keys(block))
        od_ref[which] = od_ref[which] + jnp.where(low, oq[:half], oq[half:])
        acc_ref[block] = acc_ref[block] + dot_n(lhs_t_ref[which], dsp)
    gain = jnp.where(low, scale, 1.0)
    od_a_ref[...] = (od_ref[0] * gain).astype(jnp.bfloat16)
    od_b_ref[...] = (od_ref[1] * gain).astype(jnp.bfloat16)
    dkv_ref[...] = acc_ref[...].astype(jnp.bfloat16)


def short_call(chip, mine, late, kv):
    half = late.shape[0]
    kb = 2 * half
    blocks = kv.shape[0] // kb
    vm = pl.BlockSpec(memory_space=pltpu.VMEM)
    f32, bf16 = jnp.float32, jnp.bfloat16
    return pl.pallas_call(
        short_kernel,
        out_shape=(jax.ShapeDtypeStruct((half, LANES), bf16),
                   jax.ShapeDtypeStruct((half, LANES), bf16),
                   jax.ShapeDtypeStruct((blocks, LANES, kb), bf16)),
        in_specs=[pl.BlockSpec(memory_space=pltpu.SMEM), vm, vm, vm],
        out_specs=(vm, vm, vm),
        scratch_shapes=[
            pltpu.VMEM((2, kb, LANES), bf16),
            pltpu.VMEM((2, LANES, kb), bf16),
            pltpu.VMEM((blocks + 1, half, kb), f32),
            pltpu.VMEM((blocks + 1, half, kb), f32),
            pltpu.VMEM((2, half, LANES), f32),
            pltpu.VMEM((2, half, LANES), f32),
            pltpu.VMEM((2, half, LANES), f32),
            pltpu.VMEM((2, half, LANES), f32),
            pltpu.VMEM((blocks, LANES, kb), f32),
        ],
        compiler_params=pltpu.CompilerParams(vmem_limit_bytes=32 * 1024 * 1024),
        cost_estimate=pl.CostEstimate(
            flops=6 * (blocks + 1) * half * kb * LANES * 2, bytes_accessed=4 * blocks * kb * LANES,
            transcendentals=(blocks + 1) * half * kb),
        name="short_layer",
    )(chip, mine, late, kv)


def reduce_kernel(core_ref, parts_ref, od_a_ref, od_b_ref, keep_ref, give_ref):
    half = keep_ref.shape[0]
    total = parts_ref[0].astype(jnp.float32)
    for i in range(1, parts_ref.shape[0]):
        total = total + parts_ref[i].astype(jnp.float32)
    dkv = total.T.astype(jnp.bfloat16)
    first = jnp.concatenate([od_a_ref[...], dkv[:half]], axis=1)
    second = jnp.concatenate([od_b_ref[...], dkv[half:]], axis=1)
    is_first = core_ref[0] == 0
    keep_ref[...] = jnp.where(is_first, first, second)
    give_ref[...] = jnp.where(is_first, second, first)


def reduce_call(core, parts, od_a, od_b):
    half = od_a.shape[0]
    vm = pl.BlockSpec(memory_space=pltpu.VMEM)
    shape = jax.ShapeDtypeStruct((half, 2 * LANES), jnp.bfloat16)
    return pl.pallas_call(
        reduce_kernel,
        out_shape=(shape, shape),
        in_specs=[pl.BlockSpec(memory_space=pltpu.SMEM), vm, vm, vm],
        out_specs=(vm, vm),
        name="sum_terms",
    )(core, parts, od_a, od_b)


def join_kernel(core_ref, keep_ref, got_ref, out_ref, dq_ref, dk_ref, dv_ref):
    half = keep_ref.shape[0]
    low = lax.broadcasted_iota(jnp.int32, (half, LANES), 1) < HD
    is_first = core_ref[0] == 0
    keep = keep_ref[...].astype(jnp.float32)
    got = got_ref[...].astype(jnp.float32)
    even = jnp.where(is_first, keep, got)
    odd = jnp.where(is_first, got, keep)
    for part, (left, right) in enumerate(((dq_ref, out_ref), (dk_ref, dv_ref))):
        cols = slice(part * LANES, (part + 1) * LANES)
        a, b = even[:, cols], odd[:, cols]
        left[...] = jnp.where(low, a, pltpu.roll(b, HD, 1)).astype(jnp.bfloat16)
        right[...] = jnp.where(low, pltpu.roll(a, HD, 1), b).astype(jnp.bfloat16)


def join_call(core, keep, got):
    vm = pl.BlockSpec(memory_space=pltpu.VMEM)
    shape = jax.ShapeDtypeStruct((keep.shape[0], LANES), jnp.bfloat16)
    return pl.pallas_call(
        join_kernel,
        out_shape=(shape,) * 4,
        in_specs=[pl.BlockSpec(memory_space=pltpu.SMEM), vm, vm],
        out_specs=(vm,) * 4,
        name="join_heads",
    )(core, keep, got)


def on_device(sizes, q_local, k_local, v_local, q_short, k_short, v_short, grad_out):
    nx, ny, nc, nz = sizes
    axes = ("x", "y", "c", "z")
    count = nx * ny * nc * nz
    chips = nx * ny
    me = lax.axis_index(axes).astype(jnp.int32)[None]
    chip = lax.axis_index(("x", "y")).astype(jnp.int32)[None]
    core = lax.axis_index("c").astype(jnp.int32)[None]
    mirror = [(i, chips - 1 - i) for i in range(chips)]

    packed = pack_call(q_short, k_short, v_short, grad_out)
    mine = lax.all_to_all(packed, ("c", "z"), split_axis=0, concat_axis=0, tiled=True)
    mine = mine.reshape(-1, 4 * HD)
    spread, late = spread_call(mine, chips)
    kv = lax.all_to_all(spread, ("x", "y"), split_axis=0, concat_axis=0, tiled=True)
    kv = kv.reshape(-1, LANES)
    late = lax.ppermute(late, ("x", "y"), mirror)

    down = [(i, i + 1) for i in range(count - 1)]
    up = [(i + 1, i) for i in range(count - 1)]
    k_sent, v_sent, _ = lax.optimization_barrier((k_local, v_local, mine))
    prev_k = lax.ppermute(k_sent, axes, down)
    prev_v = lax.ppermute(v_sent, axes, down)

    kv, late, prev_k, prev_v = lax.optimization_barrier((kv, late, prev_k, prev_v))
    od_a, od_b, dkv = short_call(chip, mine, late, kv)
    parts = lax.all_to_all(dkv, ("x", "y"), split_axis=0, concat_axis=0, tiled=True)
    od_b = lax.ppermute(od_b, ("x", "y"), mirror)

    prev_k, prev_v, od_a = lax.optimization_barrier((prev_k, prev_v, od_a))
    local_out, local_dq, own_k, own_v, back_k, back_v = local_call(
        me, q_local, k_local, v_local, grad_out, prev_k, prev_v)
    back_k = lax.ppermute(back_k, axes, up)
    back_v = lax.ppermute(back_v, axes, up)
    local_dk = (own_k + back_k.astype(jnp.float32)).astype(jnp.bfloat16)
    local_dv = (own_v + back_v.astype(jnp.float32)).astype(jnp.bfloat16)

    keep, give = reduce_call(core, parts, od_a, od_b)
    got = lax.ppermute(give, "c", [(0, 1), (1, 0)])
    short_out, short_dq, short_dk, short_dv = join_call(core, keep, got)
    return (local_out, local_dq, local_dk, local_dv, short_out, short_dq, short_dk, short_dv)


def solution(mesh):
    nx, ny, nc, nz = 4, 4, 2, 8
    sizes = (nx, ny, nc, nz)
    fine = Mesh(mesh.devices.reshape(sizes), ("x", "y", "c", "z"))
    rows = P(("x", "y", "c", "z"), None)
    heads = P(("x", "y", "c"), "z")

    def body(*args):
        return on_device(sizes, *args)

    return jax.shard_map(
        body,
        mesh=fine,
        in_specs=(rows,) * 7,
        out_specs=(rows,) * 4 + (heads,) * 4,
        check_vma=False,
    )
```

```python
import math

import jax
import jax.numpy as jnp
from jax import lax
from jax.experimental import pallas as pl
from jax.experimental.pallas import tpu as pltpu
from jax.sharding import Mesh
from jax.sharding import PartitionSpec as P

HD = 64
WINDOW = 128
POOL = 8
LANES = 128
NEG = float("-inf")
MIB = 1024 * 1024


def dot_t(a, b):
    return lax.dot_general(a, b, (((1,), (1,)), ((), ())), preferred_element_type=jnp.float32)


def dot_n(a, b):
    return lax.dot_general(a, b, (((1,), (0,)), ((), ())), preferred_element_type=jnp.float32)


def t_dot(a, b):
    return lax.dot_general(a, b, (((0,), (0,)), ((), ())), preferred_element_type=jnp.float32)


def split_heads(x):
    low = lax.broadcasted_iota(jnp.int32, x.shape, 1) < HD
    zero = jnp.zeros_like(x)
    return jnp.concatenate([jnp.where(low, x, zero), jnp.where(low, zero, x)], axis=0)


def scaled(x):
    return (x.astype(jnp.float32) * (1.0 / math.sqrt(HD))).astype(jnp.bfloat16)


def local_kernel(first_ref, q_ref, k_ref, v_ref, g_ref, prev_ref,
                 out_ref, dq_ref, dk_ref, dv_ref, stats_ref, stats_t_ref):
    rows, width = q_ref.shape
    scale = 1.0 / math.sqrt(HD)
    low = lax.broadcasted_iota(jnp.int32, (rows, LANES), 1) < HD
    row2 = lax.broadcasted_iota(jnp.int32, (2 * rows, rows), 0) & (rows - 1)
    col2 = lax.broadcasted_iota(jnp.int32, (2 * rows, rows), 1)
    from_prev = col2 > row2
    dead = from_prev & (first_ref[0] == 0)
    zero = jnp.zeros((2 * rows, rows), jnp.bfloat16)
    stats_t_ref[...] = jnp.zeros_like(stats_t_ref)
    pairs = width // LANES
    for pair in range(pairs):
        cols = slice(pair * LANES, (pair + 1) * LANES)
        q2 = split_heads(scaled(q_ref[:, cols]))
        g2 = split_heads(g_ref[:, cols])
        kc = jnp.concatenate([prev_ref[0, :, cols], k_ref[:, cols]], axis=0)
        vc = jnp.concatenate([prev_ref[1, :, cols], v_ref[:, cols]], axis=0)
        s_all = dot_t(q2, kc)
        s = jnp.where(from_prev, s_all[:, :rows], s_all[:, rows:])
        s = jnp.where(dead, NEG, s)
        top = jnp.max(s, axis=1, keepdims=True)
        p = jnp.exp(s - top)
        total = jnp.sum(p, axis=1, keepdims=True)
        p = p * (1.0 / total)
        pb = p.astype(jnp.bfloat16)
        own_p = jnp.where(from_prev, zero, pb)
        pc = jnp.concatenate([jnp.where(from_prev, pb, zero), own_p], axis=1)
        o2 = dot_n(pc, vc).astype(jnp.bfloat16)
        out_ref[:, cols] = jnp.where(low, o2[:rows], o2[rows:])
        dots = jnp.sum(g2.astype(jnp.float32) * o2.astype(jnp.float32), axis=1, keepdims=True)
        stats_t_ref[:, pair:pair + 1] = top + jnp.log(total)
        stats_t_ref[:, pairs + pair:pairs + pair + 1] = dots
        dp_all = dot_t(g2, vc)
        dp = jnp.where(from_prev, dp_all[:, :rows], dp_all[:, rows:])
        ds = (p * (dp - dots)).astype(jnp.bfloat16)
        own_ds = jnp.where(from_prev, zero, ds)
        dc = jnp.concatenate([jnp.where(from_prev, ds, zero), own_ds], axis=1)
        dq2 = dot_n(dc, kc) * scale
        dq_ref[:, cols] = jnp.where(low, dq2[:rows], dq2[rows:]).astype(jnp.bfloat16)
        dk_ref[:, cols] = t_dot(own_ds, q2)
        dv_ref[:, cols] = t_dot(own_p, g2)
    stats_ref[...] = stats_t_ref[...].T[:2 * pairs]


def local_call(first, q, k, v, g, prev):
    rows, width = q.shape
    wide = jax.ShapeDtypeStruct((rows, width), jnp.float32)
    half = jax.ShapeDtypeStruct((rows, width), jnp.bfloat16)
    vm = pl.BlockSpec(memory_space=pltpu.VMEM)
    return pl.pallas_call(
        local_kernel,
        out_shape=(half, half, wide, wide,
                   jax.ShapeDtypeStruct((2 * width // LANES, 2 * rows), jnp.float32)),
        in_specs=[pl.BlockSpec(memory_space=pltpu.SMEM)] + [vm] * 5,
        out_specs=(vm,) * 5,
        scratch_shapes=[pltpu.VMEM((2 * rows, LANES), jnp.float32)],
        compiler_params=pltpu.CompilerParams(vmem_limit_bytes=12 * MIB),
        cost_estimate=pl.CostEstimate(
            flops=12 * rows * 256 * width * 2, bytes_accessed=12 * rows * width * 2,
            transcendentals=rows * rows * 16),
        name="local_layer",
    )(first, q, k, v, g, prev)


def late_kernel(k_ref, v_ref, next_ref, stats_ref, own_k_ref, own_v_ref, dk_ref, dv_ref, token_ref):
    rows, width = k_ref.shape
    pairs = width // LANES
    key = lax.broadcasted_iota(jnp.int32, (rows, 2 * rows), 0)
    query = lax.broadcasted_iota(jnp.int32, (rows, 2 * rows), 1) & (rows - 1)
    seen = key > query
    token_ref[...] = jnp.zeros_like(token_ref)
    for pair in range(pairs):
        cols = slice(pair * LANES, (pair + 1) * LANES)
        q2 = split_heads(scaled(next_ref[0, :, cols]))
        g2 = split_heads(next_ref[1, :, cols])
        s = dot_t(k_ref[:, cols], q2)
        dp = dot_t(v_ref[:, cols], g2)
        lse = stats_ref[pair:pair + 1, :]
        dots = stats_ref[pairs + pair:pairs + pair + 1, :]
        p = jnp.exp(jnp.where(seen, s - lse, NEG))
        ds = p * (dp - dots)
        dk = own_k_ref[:, cols] + dot_n(ds.astype(jnp.bfloat16), q2)
        dv = own_v_ref[:, cols] + dot_n(p.astype(jnp.bfloat16), g2)
        dk_ref[:, cols] = dk.astype(jnp.bfloat16)
        dv_ref[:, cols] = dv.astype(jnp.bfloat16)


def late_call(k, v, following, stats, own_k, own_v):
    rows, width = k.shape
    half = jax.ShapeDtypeStruct((rows, width), jnp.bfloat16)
    vm = pl.BlockSpec(memory_space=pltpu.VMEM)
    return pl.pallas_call(
        late_kernel,
        out_shape=(half, half, jax.ShapeDtypeStruct((8, LANES), jnp.float32)),
        in_specs=[vm] * 6,
        out_specs=(vm,) * 3,
        compiler_params=pltpu.CompilerParams(vmem_limit_bytes=12 * MIB),
        cost_estimate=pl.CostEstimate(
            flops=8 * rows * 256 * width, bytes_accessed=12 * rows * width * 2,
            transcendentals=rows * rows * 16),
        name="late_keys",
    )(k, v, following, stats, own_k, own_v)


def pack_kernel(q_ref, k_ref, v_ref, g_ref, packed_ref):
    small = q_ref.shape[0]
    low = lax.broadcasted_iota(jnp.int32, (small, LANES), 1) < HD

    def halves(a, b):
        swap_a = pltpu.roll(a, HD, 1)
        swap_b = pltpu.roll(b, HD, 1)
        return jnp.where(low, a, swap_b), jnp.where(low, swap_a, b)

    pairs = q_ref.shape[1] // LANES
    for pair in range(pairs):
        cols = slice(pair * LANES, (pair + 1) * LANES)
        grads = g_ref[:, cols].astype(jnp.float32).reshape(small, POOL, LANES)
        pooled = jnp.sum(grads, axis=1).astype(jnp.bfloat16).astype(jnp.float32)
        quarter = [r[:, cols].astype(jnp.float32) for r in (q_ref, k_ref, v_ref)]
        qg = halves(quarter[0], pooled)
        kv = halves(quarter[1], quarter[2])
        for core in range(2):
            packed_ref[core * pairs + pair, :, :LANES] = qg[core].astype(jnp.bfloat16)
            packed_ref[core * pairs + pair, :, LANES:] = kv[core].astype(jnp.bfloat16)


def pack_call(q, k, v, g):
    small, width = q.shape
    vm = pl.BlockSpec(memory_space=pltpu.VMEM)
    return pl.pallas_call(
        pack_kernel,
        out_shape=jax.ShapeDtypeStruct((width // HD, small, 4 * HD), jnp.bfloat16),
        in_specs=[vm] * 4,
        out_specs=vm,
        name="pack_heads",
    )(q, k, v, g)


def short_kernel(chip_ref, mine_ref, kv_ref, od_ref, dkv_ref,
                 lhs_ref, lhs_t_ref, s_ref, dp_ref, top_ref, sum_ref, dot_ref, acc_ref,
                 stage_ref, sem):
    scale = 1.0 / math.sqrt(HD)
    chip = chip_ref[0]
    blocks, _, kb = stage_ref.shape
    rows = mine_ref.shape[0]
    low = lax.broadcasted_iota(jnp.int32, (rows, LANES), 1) < HD
    qg = mine_ref[:, :LANES]
    zero_b = jnp.zeros((rows, LANES), jnp.bfloat16)
    qz = jnp.where(low, (qg.astype(jnp.float32) * scale).astype(jnp.bfloat16), zero_b)
    gz = jnp.where(low, zero_b, qg)
    lhs = jnp.concatenate([qz, gz], axis=0)
    lhs_ref[...] = lhs
    lhs_t_ref[...] = lhs.T
    tri = (lax.broadcasted_iota(jnp.int32, (rows, kb), 1)
           <= lax.broadcasted_iota(jnp.int32, (rows, kb), 0))
    spots = [(chip - t) & (blocks - 1) for t in range(blocks)]
    shut = [jnp.where(chip < t, NEG, 0.0) for t in range(blocks)]
    copies = [pltpu.make_async_copy(stage_ref.at[j], dkv_ref.at[spots[j]], sem.at[j])
              for j in range(blocks)]

    def keys(t):
        return kv_ref[pl.ds(pl.multiple_of(spots[t] * kb, kb), kb), :]

    top = None
    for t in range(blocks):
        both = dot_t(lhs_ref[...], keys(t))
        s = both[:rows]
        if t == 0:
            s = jnp.where(tri, s, NEG)
        s_ref[t] = s
        dp_ref[t] = both[rows:]
        most = jnp.maximum(s[:, :LANES], s[:, LANES:])
        if t > 0:
            most = most + shut[t]
        top_ref[...] = most if t == 0 else jnp.maximum(top_ref[...], most)
    top_ref[...] = jnp.broadcast_to(jnp.max(top_ref[...], axis=1, keepdims=True), (rows, LANES))
    for t in range(blocks):
        top = top_ref[...]
        if t > 0:
            top = top - shut[t]
        e = jnp.exp(s_ref[t] - jnp.concatenate([top, top], axis=1))
        s_ref[t] = e
        ed = e * dp_ref[t]
        es = e[:, :LANES] + e[:, LANES:]
        eds = ed[:, :LANES] + ed[:, LANES:]
        sum_ref[...] = es if t == 0 else sum_ref[...] + es
        dot_ref[...] = eds if t == 0 else dot_ref[...] + eds
    inv = 1.0 / jnp.sum(sum_ref[...], axis=1, keepdims=True)
    dots = jnp.sum(dot_ref[...], axis=1, keepdims=True) * inv
    sum_ref[...] = jnp.broadcast_to(inv, (rows, LANES))
    dot_ref[...] = jnp.broadcast_to(dots, (rows, LANES))
    for t in range(blocks):
        inv, dots = sum_ref[...], dot_ref[...]
        p = s_ref[t] * jnp.concatenate([inv, inv], axis=1)
        ds = p * (dp_ref[t] - jnp.concatenate([dots, dots], axis=1))
        dsp = jnp.concatenate([ds.astype(jnp.bfloat16), p.astype(jnp.bfloat16)], axis=0)
        oq = dot_n(dsp, keys(t))
        od = jnp.where(low, oq[:rows], oq[rows:])
        acc_ref[...] = od if t == 0 else acc_ref[...] + od
        stage_ref[t] = dot_n(lhs_t_ref[...], dsp).astype(jnp.bfloat16)
        copies[t].start()
    od_ref[...] = (acc_ref[...] * jnp.where(low, scale, 1.0)).astype(jnp.bfloat16)
    for j in range(blocks):
        copies[j].wait()


def short_call(chip, mine, kv):
    rows = mine.shape[0]
    kb = rows
    blocks = kv.shape[0] // kb
    vm = pl.BlockSpec(memory_space=pltpu.VMEM)
    f32, bf16 = jnp.float32, jnp.bfloat16
    return pl.pallas_call(
        short_kernel,
        out_shape=(jax.ShapeDtypeStruct((rows, LANES), bf16),
                   jax.ShapeDtypeStruct((blocks, LANES, kb), bf16)),
        in_specs=[pl.BlockSpec(memory_space=pltpu.SMEM), vm, vm],
        out_specs=(vm, pl.BlockSpec(memory_space=pl.ANY)),
        scratch_shapes=[
            pltpu.VMEM((2 * rows, LANES), bf16),
            pltpu.VMEM((LANES, 2 * rows), bf16),
            pltpu.VMEM((blocks, rows, kb), f32),
            pltpu.VMEM((blocks, rows, kb), f32),
            pltpu.VMEM((rows, LANES), f32),
            pltpu.VMEM((rows, LANES), f32),
            pltpu.VMEM((rows, LANES), f32),
            pltpu.VMEM((rows, LANES), f32),
            pltpu.VMEM((blocks, LANES, kb), bf16),
            pltpu.SemaphoreType.DMA((blocks,)),
        ],
        compiler_params=pltpu.CompilerParams(vmem_limit_bytes=20 * MIB),
        cost_estimate=pl.CostEstimate(
            flops=rows * kb, bytes_accessed=kb, transcendentals=rows),
        name="short_layer",
    )(chip, mine, kv)


def reduce_kernel(core_ref, token_ref, parts_ref, od_ref, keep_ref, give_ref):
    half = keep_ref.shape[0]
    total = parts_ref[0].astype(jnp.float32)
    for i in range(1, parts_ref.shape[0]):
        total = total + parts_ref[i].astype(jnp.float32)
    dkv = total.T.astype(jnp.bfloat16)
    first = jnp.concatenate([od_ref[:half], dkv[:half]], axis=1)
    second = jnp.concatenate([od_ref[half:], dkv[half:]], axis=1)
    is_first = core_ref[0] == 0
    keep_ref[...] = jnp.where(is_first, first, second)
    give_ref[...] = jnp.where(is_first, second, first)


def reduce_call(core, token, parts, od):
    half = od.shape[0] // 2
    vm = pl.BlockSpec(memory_space=pltpu.VMEM)
    shape = jax.ShapeDtypeStruct((half, 2 * LANES), jnp.bfloat16)
    return pl.pallas_call(
        reduce_kernel,
        out_shape=(shape, shape),
        in_specs=[pl.BlockSpec(memory_space=pltpu.SMEM), pl.BlockSpec(memory_space=pl.ANY), vm, vm],
        out_specs=(vm, vm),
        compiler_params=pltpu.CompilerParams(vmem_limit_bytes=6 * MIB),
        name="sum_terms",
    )(core, token, parts, od)


def join_kernel(core_ref, keep_ref, got_ref, out_ref, dq_ref, dk_ref, dv_ref):
    half = keep_ref.shape[0]
    low = lax.broadcasted_iota(jnp.int32, (half, LANES), 1) < HD
    is_first = core_ref[0] == 0
    keep = keep_ref[...].astype(jnp.float32)
    got = got_ref[...].astype(jnp.float32)
    even = jnp.where(is_first, keep, got)
    odd = jnp.where(is_first, got, keep)
    for part, (left, right) in enumerate(((dq_ref, out_ref), (dk_ref, dv_ref))):
        cols = slice(part * LANES, (part + 1) * LANES)
        a, b = even[:, cols], odd[:, cols]
        left[...] = jnp.where(low, a, pltpu.roll(b, HD, 1)).astype(jnp.bfloat16)
        right[...] = jnp.where(low, pltpu.roll(a, HD, 1), b).astype(jnp.bfloat16)


def join_call(core, keep, got):
    vm = pl.BlockSpec(memory_space=pltpu.VMEM)
    shape = jax.ShapeDtypeStruct((keep.shape[0], LANES), jnp.bfloat16)
    return pl.pallas_call(
        join_kernel,
        out_shape=(shape,) * 4,
        in_specs=[pl.BlockSpec(memory_space=pltpu.SMEM), vm, vm],
        out_specs=(vm,) * 4,
        compiler_params=pltpu.CompilerParams(vmem_limit_bytes=6 * MIB),
        name="join_heads",
    )(core, keep, got)


def on_device(sizes, q_local, k_local, v_local, q_short, k_short, v_short, grad_out):
    nx, ny, nc, nz = sizes
    axes = ("x", "y", "c", "z")
    count = nx * ny * nc * nz
    chips = nx * ny
    me = lax.axis_index(axes).astype(jnp.int32)[None]
    chip = lax.axis_index(("x", "y")).astype(jnp.int32)[None]
    core = lax.axis_index("c").astype(jnp.int32)[None]

    down = [(i, i + 1) for i in range(count - 1)]
    up = [(i + 1, i) for i in range(count - 1)]
    packed = pack_call(q_short, k_short, v_short, grad_out)
    packed, k_sent, v_sent, q_sent, g_sent = lax.optimization_barrier(
        (packed, k_local, v_local, q_local, grad_out))
    mine = lax.all_to_all(packed, ("c", "z"), split_axis=0, concat_axis=0, tiled=True)
    mine = mine.reshape(-1, 4 * HD)
    halo = jnp.stack([k_sent, v_sent])
    halo_up = jnp.stack([q_sent, g_sent])
    halo, halo_up, mine = lax.optimization_barrier((halo, halo_up, mine))
    prev = lax.ppermute(halo, axes, down)
    following = lax.ppermute(halo_up, axes, up)

    chip_rows = mine.shape[0]
    spread = jnp.broadcast_to(mine[None, :, LANES:], (chips, chip_rows, LANES))
    kv = lax.all_to_all(spread, ("x", "y"), split_axis=0, concat_axis=0, tiled=True)
    kv = kv.reshape(-1, LANES)
    od, dkv = short_call(chip, mine, kv)
    dkv, prev, following = lax.optimization_barrier((dkv, prev, following))
    parts = lax.all_to_all(dkv, ("x", "y"), split_axis=0, concat_axis=0, tiled=True)
    prev, od = lax.optimization_barrier((prev, od))
    local_out, local_dq, own_k, own_v, stats = local_call(
        me, q_local, k_local, v_local, grad_out, prev)
    stats = lax.ppermute(stats, axes, up)
    local_dk, local_dv, token = late_call(k_local, v_local, following, stats, own_k, own_v)

    keep, give = reduce_call(core, token, parts, od)
    got = lax.ppermute(give, "c", [(0, 1), (1, 0)])
    short_out, short_dq, short_dk, short_dv = join_call(core, keep, got)
    return (local_out, local_dq, local_dk, local_dv, short_out, short_dq, short_dk, short_dv)


def solution(mesh):
    nx, ny, nc, nz = 4, 4, 2, 8
    sizes = (nx, ny, nc, nz)
    fine = Mesh(mesh.devices.reshape(sizes), ("x", "y", "c", "z"))
    rows = P(("x", "y", "c", "z"), None)
    heads = P(("x", "y", "c"), "z")

    def body(*args):
        return on_device(sizes, *args)

    return jax.shard_map(
        body,
        mesh=fine,
        in_specs=(rows,) * 7,
        out_specs=(rows,) * 4 + (heads,) * 4,
        check_vma=False,
    )
```

```python
import math

import jax
import jax.numpy as jnp
from jax import lax
from jax.experimental import pallas as pl
from jax.experimental.pallas import tpu as pltpu
from jax.sharding import Mesh
from jax.sharding import PartitionSpec as P

HD = 64
WINDOW = 128
POOL = 8
LANES = 128
NEG = float("-inf")
MIB = 1024 * 1024
COST = 10 ** 11


def dot_t(a, b):
    return lax.dot_general(a, b, (((1,), (1,)), ((), ())), preferred_element_type=jnp.float32)


def dot_n(a, b):
    return lax.dot_general(a, b, (((1,), (0,)), ((), ())), preferred_element_type=jnp.float32)


def t_dot(a, b):
    return lax.dot_general(a, b, (((0,), (0,)), ((), ())), preferred_element_type=jnp.float32)


def split_heads(x):
    low = lax.broadcasted_iota(jnp.int32, x.shape, 1) < HD
    zero = jnp.zeros_like(x)
    return jnp.concatenate([jnp.where(low, x, zero), jnp.where(low, zero, x)], axis=0)


def scaled(x):
    return (x.astype(jnp.float32) * (1.0 / math.sqrt(HD))).astype(jnp.bfloat16)


def weights_kernel(place_ref, q_ref, k_ref, v_ref, g_ref, prev_ref, cross_ref,
                   p_ref, ds_ref, stats_ref, s_ref, dp_ref):
    rows, width = q_ref.shape
    key = lax.broadcasted_iota(jnp.int32, (rows, 2 * rows), 0)
    query = lax.broadcasted_iota(jnp.int32, (rows, 2 * rows), 1) & (rows - 1)
    from_prev = key > query
    dead = from_prev & (place_ref[0] == 0)
    crossed = place_ref[1] == 1
    pairs = width // LANES
    for pair in range(pairs):
        cols = slice(pair * LANES, (pair + 1) * LANES)
        q2 = split_heads(scaled(q_ref[:, cols]))
        g2 = split_heads(g_ref[:, cols])
        prev_k = jnp.where(crossed, cross_ref[0, :, cols], prev_ref[0, :, cols])
        prev_v = jnp.where(crossed, cross_ref[1, :, cols], prev_ref[1, :, cols])
        s = jnp.where(from_prev, dot_t(prev_k, q2), dot_t(k_ref[:, cols], q2))
        s_ref[pair] = jnp.where(dead, NEG, s)
        dp_ref[pair] = jnp.where(
            from_prev, dot_t(prev_v, g2), dot_t(v_ref[:, cols], g2))
    for pair in range(pairs):
        s, dp = s_ref[pair], dp_ref[pair]
        top = jnp.max(s, axis=0, keepdims=True)
        e = jnp.exp(s - top)
        total = jnp.sum(e, axis=0, keepdims=True)
        inv = 1.0 / total
        dots = jnp.sum(e * dp, axis=0, keepdims=True) * inv
        p = e * inv
        p_ref[pair] = p.astype(jnp.bfloat16)
        ds_ref[pair] = (p * (dp - dots)).astype(jnp.bfloat16)
        stats_ref[pair:pair + 1, :] = top + jnp.log(total)
        stats_ref[pairs + pair:pairs + pair + 1, :] = dots


def weights_call(place, q, k, v, g, prev, cross):
    rows, width = q.shape
    pairs = width // LANES
    block = jax.ShapeDtypeStruct((pairs, rows, 2 * rows), jnp.bfloat16)
    vm = pl.BlockSpec(memory_space=pltpu.VMEM)
    return pl.pallas_call(
        weights_kernel,
        out_shape=(block, block, jax.ShapeDtypeStruct((2 * pairs, 2 * rows), jnp.float32)),
        in_specs=[pl.BlockSpec(memory_space=pltpu.SMEM)] + [vm] * 6,
        out_specs=(vm,) * 3,
        scratch_shapes=[pltpu.VMEM((pairs, rows, 2 * rows), jnp.float32)] * 2,
        compiler_params=pltpu.CompilerParams(vmem_limit_bytes=6 * MIB),
        cost_estimate=pl.CostEstimate(
            flops=COST, bytes_accessed=12 * rows * width * 2,
            transcendentals=rows * rows * 16),
        name="local_weights",
    )(place, q, k, v, g, prev, cross)


def local_kernel(place_ref, q_ref, k_ref, v_ref, g_ref, prev_ref, cross_ref, p_ref, ds_ref,
                 out_ref, dq_ref, dk_ref, dv_ref):
    rows, width = q_ref.shape
    scale = 1.0 / math.sqrt(HD)
    low = lax.broadcasted_iota(jnp.int32, (rows, LANES), 1) < HD
    query = lax.broadcasted_iota(jnp.int32, (2 * rows, rows), 0) & (rows - 1)
    key = lax.broadcasted_iota(jnp.int32, (2 * rows, rows), 1)
    from_prev = key > query
    seen = (lax.broadcasted_iota(jnp.int32, (rows, 2 * rows), 0)
            <= (lax.broadcasted_iota(jnp.int32, (rows, 2 * rows), 1) & (rows - 1)))
    zero = jnp.zeros((2 * rows, rows), jnp.bfloat16)
    zero_t = jnp.zeros((rows, 2 * rows), jnp.bfloat16)
    crossed = place_ref[1] == 1
    for pair in range(width // LANES):
        cols = slice(pair * LANES, (pair + 1) * LANES)
        q2 = split_heads(scaled(q_ref[:, cols]))
        g2 = split_heads(g_ref[:, cols])
        p_t, ds_t = p_ref[pair], ds_ref[pair]
        dk_ref[:, cols] = dot_n(jnp.where(seen, ds_t, zero_t), q2)
        dv_ref[:, cols] = dot_n(jnp.where(seen, p_t, zero_t), g2)
        prev_k = jnp.where(crossed, cross_ref[0, :, cols], prev_ref[0, :, cols])
        prev_v = jnp.where(crossed, cross_ref[1, :, cols], prev_ref[1, :, cols])
        p, ds = p_t.T, ds_t.T
        o2 = (dot_n(jnp.where(from_prev, p, zero), prev_v)
              + dot_n(jnp.where(from_prev, zero, p), v_ref[:, cols]))
        out_ref[:, cols] = jnp.where(low, o2[:rows], o2[rows:]).astype(jnp.bfloat16)
        dq2 = (dot_n(jnp.where(from_prev, ds, zero), prev_k)
               + dot_n(jnp.where(from_prev, zero, ds), k_ref[:, cols])) * scale
        dq_ref[:, cols] = jnp.where(low, dq2[:rows], dq2[rows:]).astype(jnp.bfloat16)


def local_call(place, q, k, v, g, prev, cross, p, ds):
    rows, width = q.shape
    wide = jax.ShapeDtypeStruct((rows, width), jnp.float32)
    half = jax.ShapeDtypeStruct((rows, width), jnp.bfloat16)
    vm = pl.BlockSpec(memory_space=pltpu.VMEM)
    return pl.pallas_call(
        local_kernel,
        out_shape=(half, half, wide, wide),
        in_specs=[pl.BlockSpec(memory_space=pltpu.SMEM)] + [vm] * 8,
        out_specs=(vm,) * 4,
        compiler_params=pltpu.CompilerParams(vmem_limit_bytes=6 * MIB),
        cost_estimate=pl.CostEstimate(
            flops=COST, bytes_accessed=12 * rows * width * 2,
            transcendentals=0),
        name="local_layer",
    )(place, q, k, v, g, prev, cross, p, ds)


def late_kernel(place_ref, k_ref, v_ref, next_ref, cross_ref, stats_ref, own_k_ref, own_v_ref,
                dk_ref, dv_ref, token_ref, s_ref, dp_ref):
    rows, width = k_ref.shape
    pairs = width // LANES
    key = lax.broadcasted_iota(jnp.int32, (rows, 2 * rows), 0)
    query = lax.broadcasted_iota(jnp.int32, (rows, 2 * rows), 1) & (rows - 1)
    seen = key > query
    token_ref[...] = jnp.zeros_like(token_ref)
    crossed = place_ref[2] == 1
    for pair in range(pairs):
        cols = slice(pair * LANES, (pair + 1) * LANES)
        q2 = split_heads(scaled(jnp.where(crossed, cross_ref[0, :, cols], next_ref[0, :, cols])))
        g2 = split_heads(jnp.where(crossed, cross_ref[1, :, cols], next_ref[1, :, cols]))
        s_ref[pair] = dot_t(k_ref[:, cols], q2)
        dp_ref[pair] = dot_t(v_ref[:, cols], g2)
    for pair in range(pairs):
        cols = slice(pair * LANES, (pair + 1) * LANES)
        q2 = split_heads(scaled(jnp.where(crossed, cross_ref[0, :, cols], next_ref[0, :, cols])))
        g2 = split_heads(jnp.where(crossed, cross_ref[1, :, cols], next_ref[1, :, cols]))
        lse = stats_ref[pair:pair + 1, :]
        dots = stats_ref[pairs + pair:pairs + pair + 1, :]
        p = jnp.exp(jnp.where(seen, s_ref[pair] - lse, NEG))
        ds = p * (dp_ref[pair] - dots)
        dk = own_k_ref[:, cols] + dot_n(ds.astype(jnp.bfloat16), q2)
        dv = own_v_ref[:, cols] + dot_n(p.astype(jnp.bfloat16), g2)
        dk_ref[:, cols] = dk.astype(jnp.bfloat16)
        dv_ref[:, cols] = dv.astype(jnp.bfloat16)


def late_call(place, k, v, following, cross, stats, own_k, own_v):
    rows, width = k.shape
    half = jax.ShapeDtypeStruct((rows, width), jnp.bfloat16)
    vm = pl.BlockSpec(memory_space=pltpu.VMEM)
    return pl.pallas_call(
        late_kernel,
        out_shape=(half, half, jax.ShapeDtypeStruct((8, LANES), jnp.float32)),
        in_specs=[pl.BlockSpec(memory_space=pltpu.SMEM)] + [vm] * 7,
        out_specs=(vm,) * 3,
        scratch_shapes=[pltpu.VMEM((width // LANES, rows, 2 * rows), jnp.float32)] * 2,
        compiler_params=pltpu.CompilerParams(vmem_limit_bytes=6 * MIB),
        cost_estimate=pl.CostEstimate(
            flops=COST, bytes_accessed=12 * rows * width * 2,
            transcendentals=rows * rows * 16),
        name="late_keys",
    )(place, k, v, following, cross, stats, own_k, own_v)


def pack_kernel(q_ref, k_ref, v_ref, g_ref, packed_ref):
    small = q_ref.shape[0]
    low = lax.broadcasted_iota(jnp.int32, (small, LANES), 1) < HD

    def halves(a, b):
        swap_a = pltpu.roll(a, HD, 1)
        swap_b = pltpu.roll(b, HD, 1)
        return jnp.where(low, a, swap_b), jnp.where(low, swap_a, b)

    pairs = q_ref.shape[1] // LANES
    for pair in range(pairs):
        cols = slice(pair * LANES, (pair + 1) * LANES)
        grads = g_ref[:, cols].astype(jnp.float32).reshape(small, POOL, LANES)
        pooled = jnp.sum(grads, axis=1).astype(jnp.bfloat16).astype(jnp.float32)
        quarter = [r[:, cols].astype(jnp.float32) for r in (q_ref, k_ref, v_ref)]
        qg = halves(quarter[0], pooled)
        kv = halves(quarter[1], quarter[2])
        for core in range(2):
            packed_ref[core * pairs + pair, :, :LANES] = qg[core].astype(jnp.bfloat16)
            packed_ref[core * pairs + pair, :, LANES:] = kv[core].astype(jnp.bfloat16)


def pack_call(q, k, v, g):
    small, width = q.shape
    vm = pl.BlockSpec(memory_space=pltpu.VMEM)
    return pl.pallas_call(
        pack_kernel,
        out_shape=jax.ShapeDtypeStruct((width // HD, small, 4 * HD), jnp.bfloat16),
        in_specs=[vm] * 4,
        out_specs=vm,
        name="pack_heads",
    )(q, k, v, g)


def short_kernel(chip_ref, mine_ref, kv_ref, room_ref, od_ref, dkv_ref,
                 lhs_ref, kv_t_ref, s_ref, dp_ref, acc_ref, stage_ref, sem):
    scale = 1.0 / math.sqrt(HD)
    chip = chip_ref[0]
    blocks, kb, _ = stage_ref.shape
    rows = mine_ref.shape[0]
    lhs = split_heads(mine_ref[:, :LANES])
    lhs_ref[:rows] = scaled(lhs[:rows])
    lhs_ref[rows:] = lhs[rows:]
    tri = (lax.broadcasted_iota(jnp.int32, (kb, rows), 0)
           <= lax.broadcasted_iota(jnp.int32, (kb, rows), 1))
    spots = [(chip - t) & (blocks - 1) for t in range(blocks)]
    shut = [jnp.where(chip < t, NEG, 0.0) for t in range(blocks)]
    copies = [pltpu.make_async_copy(stage_ref.at[j], dkv_ref.at[spots[j]], sem.at[j])
              for j in range(blocks)]

    def keys(t):
        return kv_ref[pl.ds(pl.multiple_of(spots[t] * kb, kb), kb), :]

    tops, sums, dot_sums = [], [], []
    for t in range(blocks):
        kv = keys(t)
        both = dot_t(kv, lhs_ref[...])
        kv_t_ref[t] = kv.T
        s, dp = both[:, :rows], both[:, rows:]
        if t == 0:
            s = jnp.where(tri, s, NEG)
        top = jnp.max(s, axis=0, keepdims=True)
        e = jnp.exp(s - top)
        s_ref[t] = e
        dp_ref[t] = dp
        tops.append(top if t == 0 else top + shut[t])
        sums.append(jnp.sum(e, axis=0, keepdims=True))
        dot_sums.append(jnp.sum(e * dp, axis=0, keepdims=True))
    top = tops[0]
    for t in range(1, blocks):
        top = jnp.maximum(top, tops[t])
    shares = [jnp.exp(each - top) for each in tops]
    inv = 1.0 / sum(share * part for share, part in zip(shares, sums))
    dots = sum(share * part for share, part in zip(shares, dot_sums)) * inv
    for t in range(blocks):
        p = s_ref[t] * (shares[t] * inv)
        ds = p * (dp_ref[t] - dots)
        dsp = jnp.concatenate([ds.astype(jnp.bfloat16), p.astype(jnp.bfloat16)], axis=1)
        stage_ref[t] = dot_n(dsp, lhs_ref[...]).astype(jnp.bfloat16)
        copies[t].start()
        od = dot_n(kv_t_ref[t], dsp)
        od = jnp.concatenate([od[:HD, :rows], od[HD:, rows:]], axis=0)
        acc_ref[...] = od if t == 0 else acc_ref[...] + od
    low = lax.broadcasted_iota(jnp.int32, (rows, LANES), 1) < HD
    od_ref[...] = (acc_ref[...].T * jnp.where(low, scale, 1.0)).astype(jnp.bfloat16)
    for copy in copies:
        copy.wait()


def short_call(chip, mine, kv, room):
    rows = mine.shape[0]
    kb = rows
    blocks = kv.shape[0] // kb
    vm = pl.BlockSpec(memory_space=pltpu.VMEM)
    f32, bf16 = jnp.float32, jnp.bfloat16
    return pl.pallas_call(
        short_kernel,
        out_shape=(jax.ShapeDtypeStruct((rows, LANES), bf16),
                   jax.ShapeDtypeStruct((blocks, kb, LANES), bf16)),
        in_specs=[pl.BlockSpec(memory_space=pltpu.SMEM), vm, vm,
                  pl.BlockSpec(memory_space=pl.ANY)],
        out_specs=(vm, pl.BlockSpec(memory_space=pl.ANY)),
        input_output_aliases={3: 1},
        scratch_shapes=[
            pltpu.VMEM((2 * rows, LANES), bf16),
            pltpu.VMEM((blocks, LANES, kb), bf16),
            pltpu.VMEM((blocks, kb, rows), f32),
            pltpu.VMEM((blocks, kb, rows), f32),
            pltpu.VMEM((LANES, rows), f32),
            pltpu.VMEM((blocks, kb, LANES), bf16),
            pltpu.SemaphoreType.DMA((blocks,)),
        ],
        compiler_params=pltpu.CompilerParams(vmem_limit_bytes=14 * MIB),
        cost_estimate=pl.CostEstimate(
            flops=rows * kb, bytes_accessed=kb, transcendentals=rows),
        name="short_layer",
    )(chip, mine, kv, room)


def reduce_kernel(core_ref, token_ref, parts_ref, od_ref, keep_ref, give_ref):
    half = keep_ref.shape[0]
    total = parts_ref[0].astype(jnp.float32)
    for i in range(1, parts_ref.shape[0]):
        total = total + parts_ref[i].astype(jnp.float32)
    dkv = total.astype(jnp.bfloat16)
    first = jnp.concatenate([od_ref[:half], dkv[:half]], axis=1)
    second = jnp.concatenate([od_ref[half:], dkv[half:]], axis=1)
    is_first = core_ref[0] == 0
    keep_ref[...] = jnp.where(is_first, first, second)
    give_ref[...] = jnp.where(is_first, second, first)


def reduce_call(core, token, parts, od):
    half = od.shape[0] // 2
    vm = pl.BlockSpec(memory_space=pltpu.VMEM)
    shape = jax.ShapeDtypeStruct((half, 2 * LANES), jnp.bfloat16)
    return pl.pallas_call(
        reduce_kernel,
        out_shape=(shape, shape),
        in_specs=[pl.BlockSpec(memory_space=pltpu.SMEM), pl.BlockSpec(memory_space=pl.ANY), vm, vm],
        out_specs=(vm, vm),
        compiler_params=pltpu.CompilerParams(vmem_limit_bytes=3 * MIB),
        name="sum_terms",
    )(core, token, parts, od)


def join_kernel(core_ref, keep_ref, got_ref, out_ref, dq_ref, dk_ref, dv_ref):
    half = keep_ref.shape[0]
    low = lax.broadcasted_iota(jnp.int32, (half, LANES), 1) < HD
    is_first = core_ref[0] == 0
    keep = keep_ref[...].astype(jnp.float32)
    got = got_ref[...].astype(jnp.float32)
    even = jnp.where(is_first, keep, got)
    odd = jnp.where(is_first, got, keep)
    for part, (left, right) in enumerate(((dq_ref, out_ref), (dk_ref, dv_ref))):
        cols = slice(part * LANES, (part + 1) * LANES)
        a, b = even[:, cols], odd[:, cols]
        left[...] = jnp.where(low, a, pltpu.roll(b, HD, 1)).astype(jnp.bfloat16)
        right[...] = jnp.where(low, pltpu.roll(a, HD, 1), b).astype(jnp.bfloat16)


def join_call(core, keep, got):
    vm = pl.BlockSpec(memory_space=pltpu.VMEM)
    shape = jax.ShapeDtypeStruct((keep.shape[0], LANES), jnp.bfloat16)
    return pl.pallas_call(
        join_kernel,
        out_shape=(shape,) * 4,
        in_specs=[pl.BlockSpec(memory_space=pltpu.SMEM), vm, vm],
        out_specs=(vm,) * 4,
        compiler_params=pltpu.CompilerParams(vmem_limit_bytes=2 * MIB),
        name="join_heads",
    )(core, keep, got)


def on_device(sizes, q_local, k_local, v_local, q_short, k_short, v_short, grad_out):
    nx, ny, nc, nz = sizes
    axes = ("x", "y", "c", "z")
    count = nx * ny * nc * nz
    chips = nx * ny
    me = lax.axis_index(axes).astype(jnp.int32)
    column = nc * nz
    is_first = me % column == 0
    is_last = me % column == column - 1
    place = jnp.stack([me, is_first.astype(jnp.int32), is_last.astype(jnp.int32)])
    chip = lax.axis_index(("x", "y")).astype(jnp.int32)[None]
    core = lax.axis_index("c").astype(jnp.int32)[None]

    steps = [(i, i + 1) for i in range(count - 1)]
    inside = [pair for pair in steps if pair[1] % column]
    across = [pair for pair in steps if pair[1] % column == 0]
    down = inside
    up = [(b, a) for a, b in inside]
    both_ways = across + [(b, a) for a, b in across]
    all_up = [(b, a) for a, b in steps]
    packed = pack_call(q_short, k_short, v_short, grad_out)
    packed, k_sent, v_sent, q_sent, g_sent = lax.optimization_barrier(
        (packed, k_local, v_local, q_local, grad_out))
    mine = lax.all_to_all(packed, ("c", "z"), split_axis=0, concat_axis=0, tiled=True)
    mine = mine.reshape(-1, 4 * HD)
    halo = jnp.stack([k_sent, v_sent])
    halo_up = jnp.stack([q_sent, g_sent])
    edge = jnp.where(is_first, halo_up, halo)
    halo, halo_up, edge, mine = lax.optimization_barrier((halo, halo_up, edge, mine))
    prev = lax.ppermute(halo, axes, down)
    following = lax.ppermute(halo_up, axes, up)

    chip_rows = mine.shape[0]
    spread = jnp.broadcast_to(mine[None, :, LANES:], (chips, chip_rows, LANES))
    kv = lax.all_to_all(spread, ("x", "y"), split_axis=0, concat_axis=0, tiled=True)
    kv = kv.reshape(-1, LANES)
    cross = lax.ppermute(edge, axes, both_ways)
    od, dkv = short_call(chip, mine, kv, spread)
    dkv, prev, following, cross = lax.optimization_barrier((dkv, prev, following, cross))
    parts = lax.all_to_all(dkv, ("x", "y"), split_axis=0, concat_axis=0, tiled=True)
    prev, od = lax.optimization_barrier((prev, od))
    weights, dscore, stats = weights_call(
        place, q_local, k_local, v_local, grad_out, prev, cross)
    stats = lax.ppermute(stats, axes, all_up)
    local_out, local_dq, own_k, own_v = local_call(
        place, q_local, k_local, v_local, grad_out, prev, cross, weights, dscore)
    local_dk, local_dv, token = late_call(
        place, k_local, v_local, following, cross, stats, own_k, own_v)

    keep, give = reduce_call(core, token, parts, od)
    got = lax.ppermute(give, "c", [(0, 1), (1, 0)])
    short_out, short_dq, short_dk, short_dv = join_call(core, keep, got)
    return (local_out, local_dq, local_dk, local_dv, short_out, short_dq, short_dk, short_dv)


def solution(mesh):
    nx, ny, nc, nz = 4, 4, 2, 8
    sizes = (nx, ny, nc, nz)
    fine = Mesh(mesh.devices.reshape(sizes), ("x", "y", "c", "z"))
    rows = P(("x", "y", "c", "z"), None)
    heads = P(("x", "y", "c"), "z")

    def body(*args):
        return on_device(sizes, *args)

    return jax.shard_map(
        body,
        mesh=fine,
        in_specs=(rows,) * 7,
        out_specs=(rows,) * 4 + (heads,) * 4,
        check_vma=False,
    )
```

```python
import math

import jax
import jax.numpy as jnp
from jax import lax
from jax.experimental import pallas as pl
from jax.experimental.pallas import tpu as pltpu
from jax.sharding import Mesh
from jax.sharding import PartitionSpec as P

HD = 64
WINDOW = 128
POOL = 8
LANES = 128
NEG = float("-inf")
MIB = 1024 * 1024


def dot_t(a, b):
    return lax.dot_general(a, b, (((1,), (1,)), ((), ())), preferred_element_type=jnp.float32)


def dot_n(a, b):
    return lax.dot_general(a, b, (((1,), (0,)), ((), ())), preferred_element_type=jnp.float32)


def t_dot(a, b):
    return lax.dot_general(a, b, (((0,), (0,)), ((), ())), preferred_element_type=jnp.float32)


def split_heads(x):
    low = lax.broadcasted_iota(jnp.int32, x.shape, 1) < HD
    zero = jnp.zeros_like(x)
    return jnp.concatenate([jnp.where(low, x, zero), jnp.where(low, zero, x)], axis=0)


def scaled(x):
    return (x.astype(jnp.float32) * (1.0 / math.sqrt(HD))).astype(jnp.bfloat16)


def weights_kernel(place_ref, q_ref, k_ref, v_ref, g_ref, prev_ref, cross_ref,
                   p_ref, ds_ref, stats_ref, s_ref, dp_ref):
    rows, width = q_ref.shape
    key = lax.broadcasted_iota(jnp.int32, (rows, 2 * rows), 0)
    query = lax.broadcasted_iota(jnp.int32, (rows, 2 * rows), 1) & (rows - 1)
    from_prev = key > query
    dead = from_prev & (place_ref[0] == 0)
    crossed = place_ref[1] == 1
    pairs = width // LANES
    for pair in range(pairs):
        cols = slice(pair * LANES, (pair + 1) * LANES)
        q2 = split_heads(scaled(q_ref[:, cols]))
        g2 = split_heads(g_ref[:, cols])
        prev_k = jnp.where(crossed, cross_ref[0, :, cols], prev_ref[0, :, cols])
        prev_v = jnp.where(crossed, cross_ref[1, :, cols], prev_ref[1, :, cols])
        s = jnp.where(from_prev, dot_t(prev_k, q2), dot_t(k_ref[:, cols], q2))
        s_ref[pair] = jnp.where(dead, NEG, s)
        dp_ref[pair] = jnp.where(
            from_prev, dot_t(prev_v, g2), dot_t(v_ref[:, cols], g2))
    for pair in range(pairs):
        s, dp = s_ref[pair], dp_ref[pair]
        top = jnp.max(s, axis=0, keepdims=True)
        e = jnp.exp(s - top)
        total = jnp.sum(e, axis=0, keepdims=True)
        inv = 1.0 / total
        dots = jnp.sum(e * dp, axis=0, keepdims=True) * inv
        p = e * inv
        p_ref[pair] = p.astype(jnp.bfloat16)
        ds_ref[pair] = (p * (dp - dots)).astype(jnp.bfloat16)
        stats_ref[pair:pair + 1, :] = top + jnp.log(total)
        stats_ref[pairs + pair:pairs + pair + 1, :] = dots


def weights_call(place, q, k, v, g, prev, cross):
    rows, width = q.shape
    pairs = width // LANES
    block = jax.ShapeDtypeStruct((pairs, rows, 2 * rows), jnp.bfloat16)
    vm = pl.BlockSpec(memory_space=pltpu.VMEM)
    return pl.pallas_call(
        weights_kernel,
        out_shape=(block, block, jax.ShapeDtypeStruct((2 * pairs, 2 * rows), jnp.float32)),
        in_specs=[pl.BlockSpec(memory_space=pltpu.SMEM)] + [vm] * 6,
        out_specs=(vm,) * 3,
        scratch_shapes=[pltpu.VMEM((pairs, rows, 2 * rows), jnp.float32)] * 2,
        compiler_params=pltpu.CompilerParams(vmem_limit_bytes=6 * MIB),
        cost_estimate=pl.CostEstimate(
            flops=8 * rows * 256 * width * 2, bytes_accessed=12 * rows * width * 2,
            transcendentals=rows * rows * 16),
        name="local_weights",
    )(place, q, k, v, g, prev, cross)


def local_kernel(place_ref, q_ref, k_ref, v_ref, g_ref, prev_ref, cross_ref, p_ref, ds_ref,
                 out_ref, dq_ref, dk_ref, dv_ref):
    rows, width = q_ref.shape
    scale = 1.0 / math.sqrt(HD)
    low = lax.broadcasted_iota(jnp.int32, (rows, LANES), 1) < HD
    query = lax.broadcasted_iota(jnp.int32, (2 * rows, rows), 0) & (rows - 1)
    key = lax.broadcasted_iota(jnp.int32, (2 * rows, rows), 1)
    from_prev = key > query
    seen = (lax.broadcasted_iota(jnp.int32, (rows, 2 * rows), 0)
            <= (lax.broadcasted_iota(jnp.int32, (rows, 2 * rows), 1) & (rows - 1)))
    zero = jnp.zeros((2 * rows, rows), jnp.bfloat16)
    zero_t = jnp.zeros((rows, 2 * rows), jnp.bfloat16)
    crossed = place_ref[1] == 1
    for pair in range(width // LANES):
        cols = slice(pair * LANES, (pair + 1) * LANES)
        q2 = split_heads(scaled(q_ref[:, cols]))
        g2 = split_heads(g_ref[:, cols])
        p_t, ds_t = p_ref[pair], ds_ref[pair]
        dk_ref[:, cols] = dot_n(jnp.where(seen, ds_t, zero_t), q2)
        dv_ref[:, cols] = dot_n(jnp.where(seen, p_t, zero_t), g2)
        prev_k = jnp.where(crossed, cross_ref[0, :, cols], prev_ref[0, :, cols])
        prev_v = jnp.where(crossed, cross_ref[1, :, cols], prev_ref[1, :, cols])
        p, ds = p_t.T, ds_t.T
        o2 = (dot_n(jnp.where(from_prev, p, zero), prev_v)
              + dot_n(jnp.where(from_prev, zero, p), v_ref[:, cols]))
        out_ref[:, cols] = jnp.where(low, o2[:rows], o2[rows:]).astype(jnp.bfloat16)
        dq2 = (dot_n(jnp.where(from_prev, ds, zero), prev_k)
               + dot_n(jnp.where(from_prev, zero, ds), k_ref[:, cols])) * scale
        dq_ref[:, cols] = jnp.where(low, dq2[:rows], dq2[rows:]).astype(jnp.bfloat16)


def local_call(place, q, k, v, g, prev, cross, p, ds):
    rows, width = q.shape
    wide = jax.ShapeDtypeStruct((rows, width), jnp.float32)
    half = jax.ShapeDtypeStruct((rows, width), jnp.bfloat16)
    vm = pl.BlockSpec(memory_space=pltpu.VMEM)
    return pl.pallas_call(
        local_kernel,
        out_shape=(half, half, wide, wide),
        in_specs=[pl.BlockSpec(memory_space=pltpu.SMEM)] + [vm] * 8,
        out_specs=(vm,) * 4,
        compiler_params=pltpu.CompilerParams(vmem_limit_bytes=6 * MIB),
        cost_estimate=pl.CostEstimate(
            flops=8 * rows * 256 * width * 2, bytes_accessed=12 * rows * width * 2,
            transcendentals=0),
        name="local_layer",
    )(place, q, k, v, g, prev, cross, p, ds)


def late_kernel(place_ref, k_ref, v_ref, next_ref, cross_ref, stats_ref, own_k_ref, own_v_ref,
                dk_ref, dv_ref, token_ref, s_ref, dp_ref):
    rows, width = k_ref.shape
    pairs = width // LANES
    key = lax.broadcasted_iota(jnp.int32, (rows, 2 * rows), 0)
    query = lax.broadcasted_iota(jnp.int32, (rows, 2 * rows), 1) & (rows - 1)
    seen = key > query
    token_ref[...] = jnp.zeros_like(token_ref)
    crossed = place_ref[2] == 1
    for pair in range(pairs):
        cols = slice(pair * LANES, (pair + 1) * LANES)
        q2 = split_heads(scaled(jnp.where(crossed, cross_ref[0, :, cols], next_ref[0, :, cols])))
        g2 = split_heads(jnp.where(crossed, cross_ref[1, :, cols], next_ref[1, :, cols]))
        s_ref[pair] = dot_t(k_ref[:, cols], q2)
        dp_ref[pair] = dot_t(v_ref[:, cols], g2)
    for pair in range(pairs):
        cols = slice(pair * LANES, (pair + 1) * LANES)
        q2 = split_heads(scaled(jnp.where(crossed, cross_ref[0, :, cols], next_ref[0, :, cols])))
        g2 = split_heads(jnp.where(crossed, cross_ref[1, :, cols], next_ref[1, :, cols]))
        lse = stats_ref[pair:pair + 1, :]
        dots = stats_ref[pairs + pair:pairs + pair + 1, :]
        p = jnp.exp(jnp.where(seen, s_ref[pair] - lse, NEG))
        ds = p * (dp_ref[pair] - dots)
        dk = own_k_ref[:, cols] + dot_n(ds.astype(jnp.bfloat16), q2)
        dv = own_v_ref[:, cols] + dot_n(p.astype(jnp.bfloat16), g2)
        dk_ref[:, cols] = dk.astype(jnp.bfloat16)
        dv_ref[:, cols] = dv.astype(jnp.bfloat16)


def late_call(place, k, v, following, cross, stats, own_k, own_v):
    rows, width = k.shape
    half = jax.ShapeDtypeStruct((rows, width), jnp.bfloat16)
    vm = pl.BlockSpec(memory_space=pltpu.VMEM)
    return pl.pallas_call(
        late_kernel,
        out_shape=(half, half, jax.ShapeDtypeStruct((8, LANES), jnp.float32)),
        in_specs=[pl.BlockSpec(memory_space=pltpu.SMEM)] + [vm] * 7,
        out_specs=(vm,) * 3,
        scratch_shapes=[pltpu.VMEM((width // LANES, rows, 2 * rows), jnp.float32)] * 2,
        compiler_params=pltpu.CompilerParams(vmem_limit_bytes=6 * MIB),
        cost_estimate=pl.CostEstimate(
            flops=8 * rows * 256 * width * 2, bytes_accessed=12 * rows * width * 2,
            transcendentals=rows * rows * 16),
        name="late_keys",
    )(place, k, v, following, cross, stats, own_k, own_v)


def pack_kernel(q_ref, k_ref, v_ref, g_ref, packed_ref):
    small = q_ref.shape[0]
    low = lax.broadcasted_iota(jnp.int32, (small, LANES), 1) < HD

    def halves(a, b):
        swap_a = pltpu.roll(a, HD, 1)
        swap_b = pltpu.roll(b, HD, 1)
        return jnp.where(low, a, swap_b), jnp.where(low, swap_a, b)

    pairs = q_ref.shape[1] // LANES
    for pair in range(pairs):
        cols = slice(pair * LANES, (pair + 1) * LANES)
        grads = g_ref[:, cols].astype(jnp.float32).reshape(small, POOL, LANES)
        pooled = jnp.sum(grads, axis=1).astype(jnp.bfloat16).astype(jnp.float32)
        quarter = [r[:, cols].astype(jnp.float32) for r in (q_ref, k_ref, v_ref)]
        qg = halves(quarter[0], pooled)
        kv = halves(quarter[1], quarter[2])
        for core in range(2):
            packed_ref[core * pairs + pair, :, :LANES] = qg[core].astype(jnp.bfloat16)
            packed_ref[core * pairs + pair, :, LANES:] = kv[core].astype(jnp.bfloat16)


def pack_call(q, k, v, g):
    small, width = q.shape
    vm = pl.BlockSpec(memory_space=pltpu.VMEM)
    return pl.pallas_call(
        pack_kernel,
        out_shape=jax.ShapeDtypeStruct((width // HD, small, 4 * HD), jnp.bfloat16),
        in_specs=[vm] * 4,
        out_specs=vm,
        name="pack_heads",
    )(q, k, v, g)


def short_kernel(chip_ref, mine_ref, kv_ref, room_ref, od_ref, dkv_ref,
                 lhs_ref, kv_t_ref, s_ref, dp_ref, acc_ref, stage_ref, sem):
    scale = 1.0 / math.sqrt(HD)
    chip = chip_ref[0]
    blocks, kb, _ = stage_ref.shape
    rows = mine_ref.shape[0]
    lhs = split_heads(mine_ref[:, :LANES])
    lhs_ref[:rows] = scaled(lhs[:rows])
    lhs_ref[rows:] = lhs[rows:]
    tri = (lax.broadcasted_iota(jnp.int32, (kb, rows), 0)
           <= lax.broadcasted_iota(jnp.int32, (kb, rows), 1))
    spots = [(chip - t) & (blocks - 1) for t in range(blocks)]
    shut = [jnp.where(chip < t, NEG, 0.0) for t in range(blocks)]
    copies = [pltpu.make_async_copy(stage_ref.at[j], dkv_ref.at[spots[j]], sem.at[j])
              for j in range(blocks)]

    def keys(t):
        return kv_ref[pl.ds(pl.multiple_of(spots[t] * kb, kb), kb), :]

    tops, sums, dot_sums = [], [], []
    for t in range(blocks):
        kv = keys(t)
        both = dot_t(kv, lhs_ref[...])
        kv_t_ref[t] = kv.T
        s, dp = both[:, :rows], both[:, rows:]
        if t == 0:
            s = jnp.where(tri, s, NEG)
        top = jnp.max(s, axis=0, keepdims=True)
        e = jnp.exp(s - top)
        s_ref[t] = e
        dp_ref[t] = dp
        tops.append(top if t == 0 else top + shut[t])
        sums.append(jnp.sum(e, axis=0, keepdims=True))
        dot_sums.append(jnp.sum(e * dp, axis=0, keepdims=True))
    top = tops[0]
    for t in range(1, blocks):
        top = jnp.maximum(top, tops[t])
    shares = [jnp.exp(each - top) for each in tops]
    inv = 1.0 / sum(share * part for share, part in zip(shares, sums))
    dots = sum(share * part for share, part in zip(shares, dot_sums)) * inv
    for t in range(blocks):
        p = s_ref[t] * (shares[t] * inv)
        ds = p * (dp_ref[t] - dots)
        dsp = jnp.concatenate([ds.astype(jnp.bfloat16), p.astype(jnp.bfloat16)], axis=1)
        stage_ref[t] = dot_n(dsp, lhs_ref[...]).astype(jnp.bfloat16)
        copies[t].start()
        od = dot_n(kv_t_ref[t], dsp)
        od = jnp.concatenate([od[:HD, :rows], od[HD:, rows:]], axis=0)
        acc_ref[...] = od if t == 0 else acc_ref[...] + od
    low = lax.broadcasted_iota(jnp.int32, (rows, LANES), 1) < HD
    od_ref[...] = (acc_ref[...].T * jnp.where(low, scale, 1.0)).astype(jnp.bfloat16)
    for copy in copies:
        copy.wait()


def short_call(chip, mine, kv, room):
    rows = mine.shape[0]
    kb = rows
    blocks = kv.shape[0] // kb
    vm = pl.BlockSpec(memory_space=pltpu.VMEM)
    f32, bf16 = jnp.float32, jnp.bfloat16
    return pl.pallas_call(
        short_kernel,
        out_shape=(jax.ShapeDtypeStruct((rows, LANES), bf16),
                   jax.ShapeDtypeStruct((blocks, kb, LANES), bf16)),
        in_specs=[pl.BlockSpec(memory_space=pltpu.SMEM), vm, vm,
                  pl.BlockSpec(memory_space=pl.ANY)],
        out_specs=(vm, pl.BlockSpec(memory_space=pl.ANY)),
        input_output_aliases={3: 1},
        scratch_shapes=[
            pltpu.VMEM((2 * rows, LANES), bf16),
            pltpu.VMEM((blocks, LANES, kb), bf16),
            pltpu.VMEM((blocks, kb, rows), f32),
            pltpu.VMEM((blocks, kb, rows), f32),
            pltpu.VMEM((LANES, rows), f32),
            pltpu.VMEM((blocks, kb, LANES), bf16),
            pltpu.SemaphoreType.DMA((blocks,)),
        ],
        compiler_params=pltpu.CompilerParams(vmem_limit_bytes=14 * MIB),
        cost_estimate=pl.CostEstimate(
            flops=rows * kb, bytes_accessed=kb, transcendentals=rows),
        name="short_layer",
    )(chip, mine, kv, room)


def reduce_kernel(core_ref, token_ref, parts_ref, od_ref, keep_ref, give_ref):
    half = keep_ref.shape[0]
    total = parts_ref[0].astype(jnp.float32)
    for i in range(1, parts_ref.shape[0]):
        total = total + parts_ref[i].astype(jnp.float32)
    dkv = total.astype(jnp.bfloat16)
    first = jnp.concatenate([od_ref[:half], dkv[:half]], axis=1)
    second = jnp.concatenate([od_ref[half:], dkv[half:]], axis=1)
    is_first = core_ref[0] == 0
    keep_ref[...] = jnp.where(is_first, first, second)
    give_ref[...] = jnp.where(is_first, second, first)


def reduce_call(core, token, parts, od):
    half = od.shape[0] // 2
    vm = pl.BlockSpec(memory_space=pltpu.VMEM)
    shape = jax.ShapeDtypeStruct((half, 2 * LANES), jnp.bfloat16)
    return pl.pallas_call(
        reduce_kernel,
        out_shape=(shape, shape),
        in_specs=[pl.BlockSpec(memory_space=pltpu.SMEM), pl.BlockSpec(memory_space=pl.ANY), vm, vm],
        out_specs=(vm, vm),
        compiler_params=pltpu.CompilerParams(vmem_limit_bytes=3 * MIB),
        name="sum_terms",
    )(core, token, parts, od)


def join_kernel(core_ref, keep_ref, got_ref, out_ref, dq_ref, dk_ref, dv_ref):
    half = keep_ref.shape[0]
    low = lax.broadcasted_iota(jnp.int32, (half, LANES), 1) < HD
    is_first = core_ref[0] == 0
    keep = keep_ref[...].astype(jnp.float32)
    got = got_ref[...].astype(jnp.float32)
    even = jnp.where(is_first, keep, got)
    odd = jnp.where(is_first, got, keep)
    for part, (left, right) in enumerate(((dq_ref, out_ref), (dk_ref, dv_ref))):
        cols = slice(part * LANES, (part + 1) * LANES)
        a, b = even[:, cols], odd[:, cols]
        left[...] = jnp.where(low, a, pltpu.roll(b, HD, 1)).astype(jnp.bfloat16)
        right[...] = jnp.where(low, pltpu.roll(a, HD, 1), b).astype(jnp.bfloat16)


def join_call(core, keep, got):
    vm = pl.BlockSpec(memory_space=pltpu.VMEM)
    shape = jax.ShapeDtypeStruct((keep.shape[0], LANES), jnp.bfloat16)
    return pl.pallas_call(
        join_kernel,
        out_shape=(shape,) * 4,
        in_specs=[pl.BlockSpec(memory_space=pltpu.SMEM), vm, vm],
        out_specs=(vm,) * 4,
        compiler_params=pltpu.CompilerParams(vmem_limit_bytes=2 * MIB),
        name="join_heads",
    )(core, keep, got)


def on_device(sizes, q_local, k_local, v_local, q_short, k_short, v_short, grad_out):
    nx, ny, nc, nz = sizes
    axes = ("x", "y", "c", "z")
    count = nx * ny * nc * nz
    chips = nx * ny
    me = lax.axis_index(axes).astype(jnp.int32)
    column = nc * nz
    is_first = me % column == 0
    is_last = me % column == column - 1
    place = jnp.stack([me, is_first.astype(jnp.int32), is_last.astype(jnp.int32)])
    chip = lax.axis_index(("x", "y")).astype(jnp.int32)[None]
    core = lax.axis_index("c").astype(jnp.int32)[None]

    steps = [(i, i + 1) for i in range(count - 1)]
    inside = [pair for pair in steps if pair[1] % column]
    across = [pair for pair in steps if pair[1] % column == 0]
    down = inside
    up = [(b, a) for a, b in inside]
    both_ways = across + [(b, a) for a, b in across]
    all_up = [(b, a) for a, b in steps]
    packed = pack_call(q_short, k_short, v_short, grad_out)
    packed, k_sent, v_sent, q_sent, g_sent = lax.optimization_barrier(
        (packed, k_local, v_local, q_local, grad_out))
    mine = lax.all_to_all(packed, ("c", "z"), split_axis=0, concat_axis=0, tiled=True)
    mine = mine.reshape(-1, 4 * HD)
    halo = jnp.stack([k_sent, v_sent])
    halo_up = jnp.stack([q_sent, g_sent])
    edge = jnp.where(is_first, halo_up, halo)
    halo, halo_up, edge, mine = lax.optimization_barrier((halo, halo_up, edge, mine))
    prev = lax.ppermute(halo, axes, down)
    following = lax.ppermute(halo_up, axes, up)

    chip_rows = mine.shape[0]
    spread = jnp.broadcast_to(mine[None, :, LANES:], (chips, chip_rows, LANES))
    kv = lax.all_to_all(spread, ("x", "y"), split_axis=0, concat_axis=0, tiled=True)
    kv = kv.reshape(-1, LANES)
    cross = lax.ppermute(edge, axes, both_ways)
    od, dkv = short_call(chip, mine, kv, spread)
    dkv, prev, following, cross = lax.optimization_barrier((dkv, prev, following, cross))
    parts = lax.all_to_all(dkv, ("x", "y"), split_axis=0, concat_axis=0, tiled=True)
    prev, od = lax.optimization_barrier((prev, od))
    weights, dscore, stats = weights_call(
        place, q_local, k_local, v_local, grad_out, prev, cross)
    stats = lax.ppermute(stats, axes, all_up)
    local_out, local_dq, own_k, own_v = local_call(
        place, q_local, k_local, v_local, grad_out, prev, cross, weights, dscore)
    local_dk, local_dv, token = late_call(
        place, k_local, v_local, following, cross, stats, own_k, own_v)

    keep, give = reduce_call(core, token, parts, od)
    got = lax.ppermute(give, "c", [(0, 1), (1, 0)])
    short_out, short_dq, short_dk, short_dv = join_call(core, keep, got)
    return (local_out, local_dq, local_dk, local_dv, short_out, short_dq, short_dk, short_dv)


def solution(mesh):
    nx, ny, nc, nz = 4, 4, 2, 8
    sizes = (nx, ny, nc, nz)
    fine = Mesh(mesh.devices.reshape(sizes), ("x", "y", "c", "z"))
    rows = P(("x", "y", "c", "z"), None)
    heads = P(("x", "y", "c"), "z")

    def body(*args):
        return on_device(sizes, *args)

    return jax.shard_map(
        body,
        mesh=fine,
        in_specs=(rows,) * 7,
        out_specs=(rows,) * 4 + (heads,) * 4,
        check_vma=False,
    )
```

```python
import math

import jax
import jax.numpy as jnp
from jax import lax
from jax.experimental import pallas as pl
from jax.experimental.pallas import tpu as pltpu
from jax.sharding import Mesh
from jax.sharding import PartitionSpec as P

HD = 64
WINDOW = 128
POOL = 8
LANES = 128
NEG = float("-inf")
MIB = 1024 * 1024


def dot_t(a, b):
    return lax.dot_general(a, b, (((1,), (1,)), ((), ())), preferred_element_type=jnp.float32)


def dot_n(a, b):
    return lax.dot_general(a, b, (((1,), (0,)), ((), ())), preferred_element_type=jnp.float32)


def t_dot(a, b):
    return lax.dot_general(a, b, (((0,), (0,)), ((), ())), preferred_element_type=jnp.float32)


def split_heads(x):
    low = lax.broadcasted_iota(jnp.int32, x.shape, 1) < HD
    zero = jnp.zeros_like(x)
    return jnp.concatenate([jnp.where(low, x, zero), jnp.where(low, zero, x)], axis=0)


def scaled(x):
    return (x.astype(jnp.float32) * (1.0 / math.sqrt(HD))).astype(jnp.bfloat16)


def weights_kernel(place_ref, q_ref, k_ref, v_ref, g_ref, prev_ref, cross_ref,
                   p_ref, ds_ref, stats_ref, s_ref, dp_ref):
    rows, width = q_ref.shape
    key = lax.broadcasted_iota(jnp.int32, (rows, 2 * rows), 0)
    query = lax.broadcasted_iota(jnp.int32, (rows, 2 * rows), 1) & (rows - 1)
    from_prev = key > query
    dead = from_prev & (place_ref[0] == 0)
    crossed = place_ref[1] == 1
    pairs = width // LANES
    for pair in range(pairs):
        cols = slice(pair * LANES, (pair + 1) * LANES)
        q2 = split_heads(scaled(q_ref[:, cols]))
        g2 = split_heads(g_ref[:, cols])
        prev_k = jnp.where(crossed, cross_ref[0, :, cols], prev_ref[0, :, cols])
        prev_v = jnp.where(crossed, cross_ref[1, :, cols], prev_ref[1, :, cols])
        s = jnp.where(from_prev, dot_t(prev_k, q2), dot_t(k_ref[:, cols], q2))
        s_ref[pair] = jnp.where(dead, NEG, s)
        dp_ref[pair] = jnp.where(
            from_prev, dot_t(prev_v, g2), dot_t(v_ref[:, cols], g2))
    for pair in range(pairs):
        s, dp = s_ref[pair], dp_ref[pair]
        top = jnp.max(s, axis=0, keepdims=True)
        e = jnp.exp(s - top)
        total = jnp.sum(e, axis=0, keepdims=True)
        inv = 1.0 / total
        dots = jnp.sum(e * dp, axis=0, keepdims=True) * inv
        p = e * inv
        p_ref[pair] = p.astype(jnp.bfloat16)
        ds_ref[pair] = (p * (dp - dots)).astype(jnp.bfloat16)
        stats_ref[pair:pair + 1, :] = top + jnp.log(total)
        stats_ref[pairs + pair:pairs + pair + 1, :] = dots


def weights_call(place, q, k, v, g, prev, cross):
    rows, width = q.shape
    pairs = width // LANES
    block = jax.ShapeDtypeStruct((pairs, rows, 2 * rows), jnp.bfloat16)
    vm = pl.BlockSpec(memory_space=pltpu.VMEM)
    return pl.pallas_call(
        weights_kernel,
        out_shape=(block, block, jax.ShapeDtypeStruct((2 * pairs, 2 * rows), jnp.float32)),
        in_specs=[pl.BlockSpec(memory_space=pltpu.SMEM)] + [vm] * 6,
        out_specs=(vm,) * 3,
        scratch_shapes=[pltpu.VMEM((pairs, rows, 2 * rows), jnp.float32)] * 2,
        compiler_params=pltpu.CompilerParams(vmem_limit_bytes=6 * MIB),
        cost_estimate=pl.CostEstimate(
            flops=8 * rows * 256 * width * 2, bytes_accessed=12 * rows * width * 2,
            transcendentals=rows * rows * 16),
        name="local_weights",
    )(place, q, k, v, g, prev, cross)


def local_kernel(place_ref, q_ref, k_ref, v_ref, g_ref, prev_ref, cross_ref, p_ref, ds_ref,
                 out_ref, dq_ref, dk_ref, dv_ref):
    rows, width = q_ref.shape
    scale = 1.0 / math.sqrt(HD)
    low = lax.broadcasted_iota(jnp.int32, (rows, LANES), 1) < HD
    query = lax.broadcasted_iota(jnp.int32, (2 * rows, rows), 0) & (rows - 1)
    key = lax.broadcasted_iota(jnp.int32, (2 * rows, rows), 1)
    from_prev = key > query
    seen = (lax.broadcasted_iota(jnp.int32, (rows, 2 * rows), 0)
            <= (lax.broadcasted_iota(jnp.int32, (rows, 2 * rows), 1) & (rows - 1)))
    zero = jnp.zeros((2 * rows, rows), jnp.bfloat16)
    zero_t = jnp.zeros((rows, 2 * rows), jnp.bfloat16)
    crossed = place_ref[1] == 1
    for pair in range(width // LANES):
        cols = slice(pair * LANES, (pair + 1) * LANES)
        q2 = split_heads(scaled(q_ref[:, cols]))
        g2 = split_heads(g_ref[:, cols])
        p_t, ds_t = p_ref[pair], ds_ref[pair]
        dk_ref[:, cols] = dot_n(jnp.where(seen, ds_t, zero_t), q2)
        dv_ref[:, cols] = dot_n(jnp.where(seen, p_t, zero_t), g2)
        prev_k = jnp.where(crossed, cross_ref[0, :, cols], prev_ref[0, :, cols])
        prev_v = jnp.where(crossed, cross_ref[1, :, cols], prev_ref[1, :, cols])
        p, ds = p_t.T, ds_t.T
        o2 = (dot_n(jnp.where(from_prev, p, zero), prev_v)
              + dot_n(jnp.where(from_prev, zero, p), v_ref[:, cols]))
        out_ref[:, cols] = jnp.where(low, o2[:rows], o2[rows:]).astype(jnp.bfloat16)
        dq2 = (dot_n(jnp.where(from_prev, ds, zero), prev_k)
               + dot_n(jnp.where(from_prev, zero, ds), k_ref[:, cols])) * scale
        dq_ref[:, cols] = jnp.where(low, dq2[:rows], dq2[rows:]).astype(jnp.bfloat16)


def local_call(place, q, k, v, g, prev, cross, p, ds):
    rows, width = q.shape
    wide = jax.ShapeDtypeStruct((rows, width), jnp.float32)
    half = jax.ShapeDtypeStruct((rows, width), jnp.bfloat16)
    vm = pl.BlockSpec(memory_space=pltpu.VMEM)
    return pl.pallas_call(
        local_kernel,
        out_shape=(half, half, wide, wide),
        in_specs=[pl.BlockSpec(memory_space=pltpu.SMEM)] + [vm] * 8,
        out_specs=(vm,) * 4,
        compiler_params=pltpu.CompilerParams(vmem_limit_bytes=6 * MIB),
        cost_estimate=pl.CostEstimate(
            flops=8 * rows * 256 * width * 2, bytes_accessed=12 * rows * width * 2,
            transcendentals=0),
        name="local_layer",
    )(place, q, k, v, g, prev, cross, p, ds)


def late_kernel(place_ref, k_ref, v_ref, next_ref, cross_ref, stats_ref, own_k_ref, own_v_ref,
                dk_ref, dv_ref, token_ref, s_ref, dp_ref):
    rows, width = k_ref.shape
    pairs = width // LANES
    key = lax.broadcasted_iota(jnp.int32, (rows, 2 * rows), 0)
    query = lax.broadcasted_iota(jnp.int32, (rows, 2 * rows), 1) & (rows - 1)
    seen = key > query
    token_ref[...] = jnp.zeros_like(token_ref)
    crossed = place_ref[2] == 1
    for pair in range(pairs):
        cols = slice(pair * LANES, (pair + 1) * LANES)
        q2 = split_heads(scaled(jnp.where(crossed, cross_ref[0, :, cols], next_ref[0, :, cols])))
        g2 = split_heads(jnp.where(crossed, cross_ref[1, :, cols], next_ref[1, :, cols]))
        s_ref[pair] = dot_t(k_ref[:, cols], q2)
        dp_ref[pair] = dot_t(v_ref[:, cols], g2)
    for pair in range(pairs):
        cols = slice(pair * LANES, (pair + 1) * LANES)
        q2 = split_heads(scaled(jnp.where(crossed, cross_ref[0, :, cols], next_ref[0, :, cols])))
        g2 = split_heads(jnp.where(crossed, cross_ref[1, :, cols], next_ref[1, :, cols]))
        lse = stats_ref[pair:pair + 1, :]
        dots = stats_ref[pairs + pair:pairs + pair + 1, :]
        p = jnp.exp(jnp.where(seen, s_ref[pair] - lse, NEG))
        ds = p * (dp_ref[pair] - dots)
        dk = own_k_ref[:, cols] + dot_n(ds.astype(jnp.bfloat16), q2)
        dv = own_v_ref[:, cols] + dot_n(p.astype(jnp.bfloat16), g2)
        dk_ref[:, cols] = dk.astype(jnp.bfloat16)
        dv_ref[:, cols] = dv.astype(jnp.bfloat16)


def late_call(place, k, v, following, cross, stats, own_k, own_v):
    rows, width = k.shape
    half = jax.ShapeDtypeStruct((rows, width), jnp.bfloat16)
    vm = pl.BlockSpec(memory_space=pltpu.VMEM)
    return pl.pallas_call(
        late_kernel,
        out_shape=(half, half, jax.ShapeDtypeStruct((8, LANES), jnp.float32)),
        in_specs=[pl.BlockSpec(memory_space=pltpu.SMEM)] + [vm] * 7,
        out_specs=(vm,) * 3,
        scratch_shapes=[pltpu.VMEM((width // LANES, rows, 2 * rows), jnp.float32)] * 2,
        compiler_params=pltpu.CompilerParams(vmem_limit_bytes=6 * MIB),
        cost_estimate=pl.CostEstimate(
            flops=8 * rows * 256 * width * 2, bytes_accessed=12 * rows * width * 2,
            transcendentals=rows * rows * 16),
        name="late_keys",
    )(place, k, v, following, cross, stats, own_k, own_v)


def pack_kernel(q_ref, k_ref, v_ref, g_ref, packed_ref):
    small = q_ref.shape[0]
    low = lax.broadcasted_iota(jnp.int32, (small, LANES), 1) < HD

    def halves(a, b):
        swap_a = pltpu.roll(a, HD, 1)
        swap_b = pltpu.roll(b, HD, 1)
        return jnp.where(low, a, swap_b), jnp.where(low, swap_a, b)

    pairs = q_ref.shape[1] // LANES
    for pair in range(pairs):
        cols = slice(pair * LANES, (pair + 1) * LANES)
        grads = g_ref[:, cols].astype(jnp.float32).reshape(small, POOL, LANES)
        pooled = jnp.sum(grads, axis=1).astype(jnp.bfloat16).astype(jnp.float32)
        quarter = [r[:, cols].astype(jnp.float32) for r in (q_ref, k_ref, v_ref)]
        qg = halves(quarter[0], pooled)
        kv = halves(quarter[1], quarter[2])
        for core in range(2):
            packed_ref[core * pairs + pair, :, :LANES] = qg[core].astype(jnp.bfloat16)
            packed_ref[core * pairs + pair, :, LANES:] = kv[core].astype(jnp.bfloat16)


def pack_call(q, k, v, g):
    small, width = q.shape
    vm = pl.BlockSpec(memory_space=pltpu.VMEM)
    return pl.pallas_call(
        pack_kernel,
        out_shape=jax.ShapeDtypeStruct((width // HD, small, 4 * HD), jnp.bfloat16),
        in_specs=[vm] * 4,
        out_specs=vm,
        name="pack_heads",
    )(q, k, v, g)


def short_kernel(chip_ref, mine_ref, kv_ref, room_ref, od_ref, dkv_ref,
                 lhs_ref, kv_t_ref, s_ref, dp_ref, acc_ref, stage_ref, sem):
    scale = 1.0 / math.sqrt(HD)
    chip = chip_ref[0]
    blocks, kb, _ = stage_ref.shape
    rows = mine_ref.shape[0]
    lhs = split_heads(mine_ref[:, :LANES])
    lhs_ref[:rows] = scaled(lhs[:rows])
    lhs_ref[rows:] = lhs[rows:]
    tri = (lax.broadcasted_iota(jnp.int32, (kb, rows), 0)
           <= lax.broadcasted_iota(jnp.int32, (kb, rows), 1))
    spots = [(chip - t) & (blocks - 1) for t in range(blocks)]
    shut = [jnp.where(chip < t, NEG, 0.0) for t in range(blocks)]
    copies = [pltpu.make_async_copy(stage_ref.at[j], dkv_ref.at[spots[j]], sem.at[j])
              for j in range(blocks)]

    def keys(t):
        return kv_ref[pl.ds(pl.multiple_of(spots[t] * kb, kb), kb), :]

    tops, sums, dot_sums = [], [], []
    for t in range(blocks):
        kv = keys(t)
        both = dot_t(kv, lhs_ref[...])
        kv_t_ref[t] = kv.T
        s, dp = both[:, :rows], both[:, rows:]
        if t == 0:
            s = jnp.where(tri, s, NEG)
        top = jnp.max(s, axis=0, keepdims=True)
        e = jnp.exp(s - top)
        s_ref[t] = e
        dp_ref[t] = dp
        tops.append(top if t == 0 else top + shut[t])
        sums.append(jnp.sum(e, axis=0, keepdims=True))
        dot_sums.append(jnp.sum(e * dp, axis=0, keepdims=True))
    top = tops[0]
    for t in range(1, blocks):
        top = jnp.maximum(top, tops[t])
    shares = [jnp.exp(each - top) for each in tops]
    inv = 1.0 / sum(share * part for share, part in zip(shares, sums))
    dots = sum(share * part for share, part in zip(shares, dot_sums)) * inv
    for t in range(blocks):
        p = s_ref[t] * (shares[t] * inv)
        ds = p * (dp_ref[t] - dots)
        dsp = jnp.concatenate([ds.astype(jnp.bfloat16), p.astype(jnp.bfloat16)], axis=1)
        stage_ref[t] = dot_n(dsp, lhs_ref[...]).astype(jnp.bfloat16)
        copies[t].start()
        od = jnp.concatenate([dot_n(kv_t_ref[t, :HD], dsp[:, :rows]),
                              dot_n(kv_t_ref[t, HD:], dsp[:, rows:])], axis=0)
        acc_ref[...] = od if t == 0 else acc_ref[...] + od
    low = lax.broadcasted_iota(jnp.int32, (rows, LANES), 1) < HD
    od_ref[...] = (acc_ref[...].T * jnp.where(low, scale, 1.0)).astype(jnp.bfloat16)
    for copy in copies:
        copy.wait()


def short_call(chip, mine, kv, room):
    rows = mine.shape[0]
    kb = rows
    blocks = kv.shape[0] // kb
    vm = pl.BlockSpec(memory_space=pltpu.VMEM)
    f32, bf16 = jnp.float32, jnp.bfloat16
    return pl.pallas_call(
        short_kernel,
        out_shape=(jax.ShapeDtypeStruct((rows, LANES), bf16),
                   jax.ShapeDtypeStruct((blocks, kb, LANES), bf16)),
        in_specs=[pl.BlockSpec(memory_space=pltpu.SMEM), vm, vm,
                  pl.BlockSpec(memory_space=pl.ANY)],
        out_specs=(vm, pl.BlockSpec(memory_space=pl.ANY)),
        input_output_aliases={3: 1},
        scratch_shapes=[
            pltpu.VMEM((2 * rows, LANES), bf16),
            pltpu.VMEM((blocks, LANES, kb), bf16),
            pltpu.VMEM((blocks, kb, rows), f32),
            pltpu.VMEM((blocks, kb, rows), f32),
            pltpu.VMEM((LANES, rows), f32),
            pltpu.VMEM((blocks, kb, LANES), bf16),
            pltpu.SemaphoreType.DMA((blocks,)),
        ],
        compiler_params=pltpu.CompilerParams(vmem_limit_bytes=14 * MIB),
        cost_estimate=pl.CostEstimate(
            flops=rows * kb, bytes_accessed=kb, transcendentals=rows),
        name="short_layer",
    )(chip, mine, kv, room)


def reduce_kernel(core_ref, token_ref, parts_ref, od_ref, keep_ref, give_ref):
    half = keep_ref.shape[0]
    total = parts_ref[0].astype(jnp.float32)
    for i in range(1, parts_ref.shape[0]):
        total = total + parts_ref[i].astype(jnp.float32)
    dkv = total.astype(jnp.bfloat16)
    first = jnp.concatenate([od_ref[:half], dkv[:half]], axis=1)
    second = jnp.concatenate([od_ref[half:], dkv[half:]], axis=1)
    is_first = core_ref[0] == 0
    keep_ref[...] = jnp.where(is_first, first, second)
    give_ref[...] = jnp.where(is_first, second, first)


def reduce_call(core, token, parts, od):
    half = od.shape[0] // 2
    vm = pl.BlockSpec(memory_space=pltpu.VMEM)
    shape = jax.ShapeDtypeStruct((half, 2 * LANES), jnp.bfloat16)
    return pl.pallas_call(
        reduce_kernel,
        out_shape=(shape, shape),
        in_specs=[pl.BlockSpec(memory_space=pltpu.SMEM), pl.BlockSpec(memory_space=pl.ANY), vm, vm],
        out_specs=(vm, vm),
        compiler_params=pltpu.CompilerParams(vmem_limit_bytes=3 * MIB),
        name="sum_terms",
    )(core, token, parts, od)


def join_kernel(core_ref, keep_ref, got_ref, out_ref, dq_ref, dk_ref, dv_ref):
    half = keep_ref.shape[0]
    low = lax.broadcasted_iota(jnp.int32, (half, LANES), 1) < HD
    is_first = core_ref[0] == 0
    keep = keep_ref[...].astype(jnp.float32)
    got = got_ref[...].astype(jnp.float32)
    even = jnp.where(is_first, keep, got)
    odd = jnp.where(is_first, got, keep)
    for part, (left, right) in enumerate(((dq_ref, out_ref), (dk_ref, dv_ref))):
        cols = slice(part * LANES, (part + 1) * LANES)
        a, b = even[:, cols], odd[:, cols]
        left[...] = jnp.where(low, a, pltpu.roll(b, HD, 1)).astype(jnp.bfloat16)
        right[...] = jnp.where(low, pltpu.roll(a, HD, 1), b).astype(jnp.bfloat16)


def join_call(core, keep, got):
    vm = pl.BlockSpec(memory_space=pltpu.VMEM)
    shape = jax.ShapeDtypeStruct((keep.shape[0], LANES), jnp.bfloat16)
    return pl.pallas_call(
        join_kernel,
        out_shape=(shape,) * 4,
        in_specs=[pl.BlockSpec(memory_space=pltpu.SMEM), vm, vm],
        out_specs=(vm,) * 4,
        compiler_params=pltpu.CompilerParams(vmem_limit_bytes=2 * MIB),
        name="join_heads",
    )(core, keep, got)


def on_device(sizes, q_local, k_local, v_local, q_short, k_short, v_short, grad_out):
    nx, ny, nc, nz = sizes
    axes = ("x", "y", "c", "z")
    count = nx * ny * nc * nz
    chips = nx * ny
    me = lax.axis_index(axes).astype(jnp.int32)
    column = nc * nz
    is_first = me % column == 0
    is_last = me % column == column - 1
    place = jnp.stack([me, is_first.astype(jnp.int32), is_last.astype(jnp.int32)])
    chip = lax.axis_index(("x", "y")).astype(jnp.int32)[None]
    core = lax.axis_index("c").astype(jnp.int32)[None]

    steps = [(i, i + 1) for i in range(count - 1)]
    inside = [pair for pair in steps if pair[1] % column]
    across = [pair for pair in steps if pair[1] % column == 0]
    down = inside
    up = [(b, a) for a, b in inside]
    both_ways = across + [(b, a) for a, b in across]
    all_up = [(b, a) for a, b in steps]
    packed = pack_call(q_short, k_short, v_short, grad_out)
    packed, k_sent, v_sent, q_sent, g_sent = lax.optimization_barrier(
        (packed, k_local, v_local, q_local, grad_out))
    mine = lax.all_to_all(packed, ("c", "z"), split_axis=0, concat_axis=0, tiled=True)
    mine = mine.reshape(-1, 4 * HD)
    halo = jnp.stack([k_sent, v_sent])
    halo_up = jnp.stack([q_sent, g_sent])
    edge = jnp.where(is_first, halo_up, halo)
    halo, halo_up, edge, mine = lax.optimization_barrier((halo, halo_up, edge, mine))
    prev = lax.ppermute(halo, axes, down)
    following = lax.ppermute(halo_up, axes, up)

    chip_rows = mine.shape[0]
    spread = jnp.broadcast_to(mine[None, :, LANES:], (chips, chip_rows, LANES))
    kv = lax.all_to_all(spread, ("x", "y"), split_axis=0, concat_axis=0, tiled=True)
    kv = kv.reshape(-1, LANES)
    cross = lax.ppermute(edge, axes, both_ways)
    od, dkv = short_call(chip, mine, kv, spread)
    dkv, prev, following, cross = lax.optimization_barrier((dkv, prev, following, cross))
    parts = lax.all_to_all(dkv, ("x", "y"), split_axis=0, concat_axis=0, tiled=True)
    prev, od = lax.optimization_barrier((prev, od))
    weights, dscore, stats = weights_call(
        place, q_local, k_local, v_local, grad_out, prev, cross)
    stats = lax.ppermute(stats, axes, all_up)
    local_out, local_dq, own_k, own_v = local_call(
        place, q_local, k_local, v_local, grad_out, prev, cross, weights, dscore)
    local_dk, local_dv, token = late_call(
        place, k_local, v_local, following, cross, stats, own_k, own_v)

    keep, give = reduce_call(core, token, parts, od)
    got = lax.ppermute(give, "c", [(0, 1), (1, 0)])
    short_out, short_dq, short_dk, short_dv = join_call(core, keep, got)
    return (local_out, local_dq, local_dk, local_dv, short_out, short_dq, short_dk, short_dv)


def solution(mesh):
    nx, ny, nc, nz = 4, 4, 2, 8
    sizes = (nx, ny, nc, nz)
    fine = Mesh(mesh.devices.reshape(sizes), ("x", "y", "c", "z"))
    rows = P(("x", "y", "c", "z"), None)
    heads = P(("x", "y", "c"), "z")

    def body(*args):
        return on_device(sizes, *args)

    return jax.shard_map(
        body,
        mesh=fine,
        in_specs=(rows,) * 7,
        out_specs=(rows,) * 4 + (heads,) * 4,
        check_vma=False,
    )
```

```python
import math

import jax
import jax.numpy as jnp
from jax import lax
from jax.experimental import pallas as pl
from jax.experimental.pallas import tpu as pltpu
from jax.sharding import Mesh
from jax.sharding import PartitionSpec as P

HD = 64
WINDOW = 128
POOL = 8
LANES = 128
NEG = float("-inf")
MIB = 1024 * 1024


def dot_t(a, b):
    return lax.dot_general(a, b, (((1,), (1,)), ((), ())), preferred_element_type=jnp.float32)


def dot_n(a, b):
    return lax.dot_general(a, b, (((1,), (0,)), ((), ())), preferred_element_type=jnp.float32)


def t_dot(a, b):
    return lax.dot_general(a, b, (((0,), (0,)), ((), ())), preferred_element_type=jnp.float32)


def split_heads(x):
    low = lax.broadcasted_iota(jnp.int32, x.shape, 1) < HD
    zero = jnp.zeros_like(x)
    return jnp.concatenate([jnp.where(low, x, zero), jnp.where(low, zero, x)], axis=0)


def scaled(x):
    return (x.astype(jnp.float32) * (1.0 / math.sqrt(HD))).astype(jnp.bfloat16)


def weights_kernel(place_ref, q_ref, k_ref, v_ref, g_ref, prev_ref, cross_ref,
                   p_ref, ds_ref, stats_ref, s_ref, dp_ref):
    rows, width = q_ref.shape
    key = lax.broadcasted_iota(jnp.int32, (rows, 2 * rows), 0)
    query = lax.broadcasted_iota(jnp.int32, (rows, 2 * rows), 1) & (rows - 1)
    from_prev = key > query
    dead = from_prev & (place_ref[0] == 0)
    crossed = place_ref[1] == 1
    pairs = width // LANES
    for pair in range(pairs):
        cols = slice(pair * LANES, (pair + 1) * LANES)
        q2 = split_heads(scaled(q_ref[:, cols]))
        g2 = split_heads(g_ref[:, cols])
        prev_k = jnp.where(crossed, cross_ref[0, :, cols], prev_ref[0, :, cols])
        prev_v = jnp.where(crossed, cross_ref[1, :, cols], prev_ref[1, :, cols])
        s = jnp.where(from_prev, dot_t(prev_k, q2), dot_t(k_ref[:, cols], q2))
        s_ref[pair] = jnp.where(dead, NEG, s)
        dp_ref[pair] = jnp.where(
            from_prev, dot_t(prev_v, g2), dot_t(v_ref[:, cols], g2))
    for pair in range(pairs):
        s, dp = s_ref[pair], dp_ref[pair]
        top = jnp.max(s, axis=0, keepdims=True)
        e = jnp.exp(s - top)
        total = jnp.sum(e, axis=0, keepdims=True)
        inv = 1.0 / total
        dots = jnp.sum(e * dp, axis=0, keepdims=True) * inv
        p = e * inv
        p_ref[pair] = p.astype(jnp.bfloat16)
        ds_ref[pair] = (p * (dp - dots)).astype(jnp.bfloat16)
        stats_ref[pair:pair + 1, :] = top + jnp.log(total)
        stats_ref[pairs + pair:pairs + pair + 1, :] = dots


def weights_call(place, q, k, v, g, prev, cross):
    rows, width = q.shape
    pairs = width // LANES
    block = jax.ShapeDtypeStruct((pairs, rows, 2 * rows), jnp.bfloat16)
    vm = pl.BlockSpec(memory_space=pltpu.VMEM)
    return pl.pallas_call(
        weights_kernel,
        out_shape=(block, block, jax.ShapeDtypeStruct((2 * pairs, 2 * rows), jnp.float32)),
        in_specs=[pl.BlockSpec(memory_space=pltpu.SMEM)] + [vm] * 6,
        out_specs=(vm,) * 3,
        scratch_shapes=[pltpu.VMEM((pairs, rows, 2 * rows), jnp.float32)] * 2,
        compiler_params=pltpu.CompilerParams(vmem_limit_bytes=6 * MIB),
        cost_estimate=pl.CostEstimate(
            flops=8 * rows * 256 * width * 2, bytes_accessed=12 * rows * width * 2,
            transcendentals=rows * rows * 16),
        name="local_weights",
    )(place, q, k, v, g, prev, cross)


def local_kernel(place_ref, q_ref, k_ref, v_ref, g_ref, prev_ref, cross_ref, p_ref, ds_ref,
                 out_ref, dq_ref, dk_ref, dv_ref):
    rows, width = q_ref.shape
    scale = 1.0 / math.sqrt(HD)
    low = lax.broadcasted_iota(jnp.int32, (rows, LANES), 1) < HD
    query = lax.broadcasted_iota(jnp.int32, (2 * rows, rows), 0) & (rows - 1)
    key = lax.broadcasted_iota(jnp.int32, (2 * rows, rows), 1)
    from_prev = key > query
    seen = (lax.broadcasted_iota(jnp.int32, (rows, 2 * rows), 0)
            <= (lax.broadcasted_iota(jnp.int32, (rows, 2 * rows), 1) & (rows - 1)))
    zero = jnp.zeros((2 * rows, rows), jnp.bfloat16)
    zero_t = jnp.zeros((rows, 2 * rows), jnp.bfloat16)
    crossed = place_ref[1] == 1
    for pair in range(width // LANES):
        cols = slice(pair * LANES, (pair + 1) * LANES)
        q2 = split_heads(scaled(q_ref[:, cols]))
        g2 = split_heads(g_ref[:, cols])
        p_t, ds_t = p_ref[pair], ds_ref[pair]
        dk_ref[:, cols] = dot_n(jnp.where(seen, ds_t, zero_t), q2)
        dv_ref[:, cols] = dot_n(jnp.where(seen, p_t, zero_t), g2)
        prev_k = jnp.where(crossed, cross_ref[0, :, cols], prev_ref[0, :, cols])
        prev_v = jnp.where(crossed, cross_ref[1, :, cols], prev_ref[1, :, cols])
        p, ds = p_t.T, ds_t.T
        o2 = (dot_n(jnp.where(from_prev, p, zero), prev_v)
              + dot_n(jnp.where(from_prev, zero, p), v_ref[:, cols]))
        out_ref[:, cols] = jnp.where(low, o2[:rows], o2[rows:]).astype(jnp.bfloat16)
        dq2 = (dot_n(jnp.where(from_prev, ds, zero), prev_k)
               + dot_n(jnp.where(from_prev, zero, ds), k_ref[:, cols])) * scale
        dq_ref[:, cols] = jnp.where(low, dq2[:rows], dq2[rows:]).astype(jnp.bfloat16)


def local_call(place, q, k, v, g, prev, cross, p, ds):
    rows, width = q.shape
    wide = jax.ShapeDtypeStruct((rows, width), jnp.float32)
    half = jax.ShapeDtypeStruct((rows, width), jnp.bfloat16)
    vm = pl.BlockSpec(memory_space=pltpu.VMEM)
    return pl.pallas_call(
        local_kernel,
        out_shape=(half, half, wide, wide),
        in_specs=[pl.BlockSpec(memory_space=pltpu.SMEM)] + [vm] * 8,
        out_specs=(vm,) * 4,
        compiler_params=pltpu.CompilerParams(vmem_limit_bytes=6 * MIB),
        cost_estimate=pl.CostEstimate(
            flops=8 * rows * 256 * width * 2, bytes_accessed=12 * rows * width * 2,
            transcendentals=0),
        name="local_layer",
    )(place, q, k, v, g, prev, cross, p, ds)


def late_kernel(place_ref, k_ref, v_ref, next_ref, cross_ref, stats_ref, own_k_ref, own_v_ref,
                dk_ref, dv_ref, token_ref, s_ref, dp_ref):
    rows, width = k_ref.shape
    pairs = width // LANES
    key = lax.broadcasted_iota(jnp.int32, (rows, 2 * rows), 0)
    query = lax.broadcasted_iota(jnp.int32, (rows, 2 * rows), 1) & (rows - 1)
    seen = key > query
    token_ref[...] = jnp.zeros_like(token_ref)
    crossed = place_ref[2] == 1
    for pair in range(pairs):
        cols = slice(pair * LANES, (pair + 1) * LANES)
        q2 = split_heads(scaled(jnp.where(crossed, cross_ref[0, :, cols], next_ref[0, :, cols])))
        g2 = split_heads(jnp.where(crossed, cross_ref[1, :, cols], next_ref[1, :, cols]))
        s_ref[pair] = dot_t(k_ref[:, cols], q2)
        dp_ref[pair] = dot_t(v_ref[:, cols], g2)
    for pair in range(pairs):
        cols = slice(pair * LANES, (pair + 1) * LANES)
        q2 = split_heads(scaled(jnp.where(crossed, cross_ref[0, :, cols], next_ref[0, :, cols])))
        g2 = split_heads(jnp.where(crossed, cross_ref[1, :, cols], next_ref[1, :, cols]))
        lse = stats_ref[pair:pair + 1, :]
        dots = stats_ref[pairs + pair:pairs + pair + 1, :]
        p = jnp.exp(jnp.where(seen, s_ref[pair] - lse, NEG))
        ds = p * (dp_ref[pair] - dots)
        dk = own_k_ref[:, cols] + dot_n(ds.astype(jnp.bfloat16), q2)
        dv = own_v_ref[:, cols] + dot_n(p.astype(jnp.bfloat16), g2)
        dk_ref[:, cols] = dk.astype(jnp.bfloat16)
        dv_ref[:, cols] = dv.astype(jnp.bfloat16)


def late_call(place, k, v, following, cross, stats, own_k, own_v):
    rows, width = k.shape
    half = jax.ShapeDtypeStruct((rows, width), jnp.bfloat16)
    vm = pl.BlockSpec(memory_space=pltpu.VMEM)
    return pl.pallas_call(
        late_kernel,
        out_shape=(half, half, jax.ShapeDtypeStruct((8, LANES), jnp.float32)),
        in_specs=[pl.BlockSpec(memory_space=pltpu.SMEM)] + [vm] * 7,
        out_specs=(vm,) * 3,
        scratch_shapes=[pltpu.VMEM((width // LANES, rows, 2 * rows), jnp.float32)] * 2,
        compiler_params=pltpu.CompilerParams(vmem_limit_bytes=6 * MIB),
        cost_estimate=pl.CostEstimate(
            flops=8 * rows * 256 * width * 2, bytes_accessed=12 * rows * width * 2,
            transcendentals=rows * rows * 16),
        name="late_keys",
    )(place, k, v, following, cross, stats, own_k, own_v)


def pack_kernel(q_ref, k_ref, v_ref, g_ref, packed_ref):
    small = q_ref.shape[0]
    low = lax.broadcasted_iota(jnp.int32, (small, LANES), 1) < HD

    def halves(a, b):
        swap_a = pltpu.roll(a, HD, 1)
        swap_b = pltpu.roll(b, HD, 1)
        return jnp.where(low, a, swap_b), jnp.where(low, swap_a, b)

    pairs = q_ref.shape[1] // LANES
    for pair in range(pairs):
        cols = slice(pair * LANES, (pair + 1) * LANES)
        grads = g_ref[:, cols].astype(jnp.float32).reshape(small, POOL, LANES)
        pooled = jnp.sum(grads, axis=1).astype(jnp.bfloat16).astype(jnp.float32)
        quarter = [r[:, cols].astype(jnp.float32) for r in (q_ref, k_ref, v_ref)]
        qg = halves(quarter[0], pooled)
        kv = halves(quarter[1], quarter[2])
        for core in range(2):
            packed_ref[core * pairs + pair, :, :LANES] = qg[core].astype(jnp.bfloat16)
            packed_ref[core * pairs + pair, :, LANES:] = kv[core].astype(jnp.bfloat16)


def pack_call(q, k, v, g):
    small, width = q.shape
    vm = pl.BlockSpec(memory_space=pltpu.VMEM)
    return pl.pallas_call(
        pack_kernel,
        out_shape=jax.ShapeDtypeStruct((width // HD, small, 4 * HD), jnp.bfloat16),
        in_specs=[vm] * 4,
        out_specs=vm,
        name="pack_heads",
    )(q, k, v, g)


def short_kernel(chip_ref, mine_ref, kv_ref, room_ref, od_ref, dkv_ref,
                 lhs_ref, kv_t_ref, s_ref, dp_ref, stage_ref, sem):
    scale = 1.0 / math.sqrt(HD)
    chip = chip_ref[0]
    blocks, kb, _ = stage_ref.shape
    rows = mine_ref.shape[0]
    lhs = split_heads(mine_ref[:, :LANES])
    lhs_ref[:rows] = scaled(lhs[:rows])
    lhs_ref[rows:] = lhs[rows:]
    tri = (lax.broadcasted_iota(jnp.int32, (kb, rows), 0)
           <= lax.broadcasted_iota(jnp.int32, (kb, rows), 1))
    spots = [(chip - t) & (blocks - 1) for t in range(blocks)]
    shut = [jnp.where(chip < t, NEG, 0.0) for t in range(blocks)]
    copies = [pltpu.make_async_copy(stage_ref.at[j], dkv_ref.at[spots[j]], sem.at[j])
              for j in range(blocks)]

    def keys(t):
        return kv_ref[pl.ds(pl.multiple_of(spots[t] * kb, kb), kb), :]

    tops, sums, dot_sums = [], [], []
    for t in range(blocks):
        kv = keys(t)
        both = dot_t(kv, lhs_ref[...])
        kv_t_ref[t] = kv.T
        s, dp = both[:, :rows], both[:, rows:]
        if t == 0:
            s = jnp.where(tri, s, NEG)
        top = jnp.max(s, axis=0, keepdims=True)
        e = jnp.exp(s - top)
        s_ref[t] = e
        dp_ref[t] = dp
        tops.append(top if t == 0 else top + shut[t])
        sums.append(jnp.sum(e, axis=0, keepdims=True))
        dot_sums.append(jnp.sum(e * dp, axis=0, keepdims=True))
    top = tops[0]
    for t in range(1, blocks):
        top = jnp.maximum(top, tops[t])
    shares = [jnp.exp(each - top) for each in tops]
    inv = 1.0 / sum(share * part for share, part in zip(shares, sums))
    dots = sum(share * part for share, part in zip(shares, dot_sums)) * inv
    for t in range(blocks):
        p = s_ref[t] * (shares[t] * inv)
        ds = p * (dp_ref[t] - dots)
        dsp = jnp.concatenate([ds.astype(jnp.bfloat16), p.astype(jnp.bfloat16)], axis=1)
        stage_ref[t] = dot_n(dsp, lhs_ref[...]).astype(jnp.bfloat16)
        copies[t].start()
        od = jnp.concatenate([dot_n(kv_t_ref[t, :HD], dsp[:, :rows]),
                              dot_n(kv_t_ref[t, HD:], dsp[:, rows:])], axis=0)
        acc = od if t == 0 else acc + od
    low = lax.broadcasted_iota(jnp.int32, (rows, LANES), 1) < HD
    od_ref[...] = (acc.T * jnp.where(low, scale, 1.0)).astype(jnp.bfloat16)
    for copy in copies:
        copy.wait()


def short_call(chip, mine, kv, room):
    rows = mine.shape[0]
    kb = rows
    blocks = kv.shape[0] // kb
    vm = pl.BlockSpec(memory_space=pltpu.VMEM)
    f32, bf16 = jnp.float32, jnp.bfloat16
    return pl.pallas_call(
        short_kernel,
        out_shape=(jax.ShapeDtypeStruct((rows, LANES), bf16),
                   jax.ShapeDtypeStruct((blocks, kb, LANES), bf16)),
        in_specs=[pl.BlockSpec(memory_space=pltpu.SMEM), vm, vm,
                  pl.BlockSpec(memory_space=pl.ANY)],
        out_specs=(vm, pl.BlockSpec(memory_space=pl.ANY)),
        input_output_aliases={3: 1},
        scratch_shapes=[
            pltpu.VMEM((2 * rows, LANES), bf16),
            pltpu.VMEM((blocks, LANES, kb), bf16),
            pltpu.VMEM((blocks, kb, rows), f32),
            pltpu.VMEM((blocks, kb, rows), f32),
            pltpu.VMEM((blocks, kb, LANES), bf16),
            pltpu.SemaphoreType.DMA((blocks,)),
        ],
        compiler_params=pltpu.CompilerParams(vmem_limit_bytes=14 * MIB),
        cost_estimate=pl.CostEstimate(
            flops=rows * kb, bytes_accessed=kb, transcendentals=rows),
        name="short_layer",
    )(chip, mine, kv, room)


def reduce_kernel(core_ref, token_ref, parts_ref, od_ref, keep_ref, give_ref):
    half = keep_ref.shape[0]
    total = parts_ref[0].astype(jnp.float32)
    for i in range(1, parts_ref.shape[0]):
        total = total + parts_ref[i].astype(jnp.float32)
    dkv = total.astype(jnp.bfloat16)
    first = jnp.concatenate([od_ref[:half], dkv[:half]], axis=1)
    second = jnp.concatenate([od_ref[half:], dkv[half:]], axis=1)
    is_first = core_ref[0] == 0
    keep_ref[...] = jnp.where(is_first, first, second)
    give_ref[...] = jnp.where(is_first, second, first)


def reduce_call(core, token, parts, od):
    half = od.shape[0] // 2
    vm = pl.BlockSpec(memory_space=pltpu.VMEM)
    shape = jax.ShapeDtypeStruct((half, 2 * LANES), jnp.bfloat16)
    return pl.pallas_call(
        reduce_kernel,
        out_shape=(shape, shape),
        in_specs=[pl.BlockSpec(memory_space=pltpu.SMEM), pl.BlockSpec(memory_space=pl.ANY), vm, vm],
        out_specs=(vm, vm),
        compiler_params=pltpu.CompilerParams(vmem_limit_bytes=3 * MIB),
        name="sum_terms",
    )(core, token, parts, od)


def join_kernel(core_ref, keep_ref, got_ref, out_ref, dq_ref, dk_ref, dv_ref):
    half = keep_ref.shape[0]
    low = lax.broadcasted_iota(jnp.int32, (half, LANES), 1) < HD
    is_first = core_ref[0] == 0
    keep = keep_ref[...].astype(jnp.float32)
    got = got_ref[...].astype(jnp.float32)
    even = jnp.where(is_first, keep, got)
    odd = jnp.where(is_first, got, keep)
    for part, (left, right) in enumerate(((dq_ref, out_ref), (dk_ref, dv_ref))):
        cols = slice(part * LANES, (part + 1) * LANES)
        a, b = even[:, cols], odd[:, cols]
        left[...] = jnp.where(low, a, pltpu.roll(b, HD, 1)).astype(jnp.bfloat16)
        right[...] = jnp.where(low, pltpu.roll(a, HD, 1), b).astype(jnp.bfloat16)


def join_call(core, keep, got):
    vm = pl.BlockSpec(memory_space=pltpu.VMEM)
    shape = jax.ShapeDtypeStruct((keep.shape[0], LANES), jnp.bfloat16)
    return pl.pallas_call(
        join_kernel,
        out_shape=(shape,) * 4,
        in_specs=[pl.BlockSpec(memory_space=pltpu.SMEM), vm, vm],
        out_specs=(vm,) * 4,
        compiler_params=pltpu.CompilerParams(vmem_limit_bytes=2 * MIB),
        name="join_heads",
    )(core, keep, got)


def on_device(sizes, q_local, k_local, v_local, q_short, k_short, v_short, grad_out):
    nx, ny, nc, nz = sizes
    axes = ("x", "y", "c", "z")
    count = nx * ny * nc * nz
    chips = nx * ny
    me = lax.axis_index(axes).astype(jnp.int32)
    column = nc * nz
    is_first = me % column == 0
    is_last = me % column == column - 1
    place = jnp.stack([me, is_first.astype(jnp.int32), is_last.astype(jnp.int32)])
    chip = lax.axis_index(("x", "y")).astype(jnp.int32)[None]
    core = lax.axis_index("c").astype(jnp.int32)[None]

    steps = [(i, i + 1) for i in range(count - 1)]
    inside = [pair for pair in steps if pair[1] % column]
    across = [pair for pair in steps if pair[1] % column == 0]
    down = inside
    up = [(b, a) for a, b in inside]
    both_ways = across + [(b, a) for a, b in across]
    all_up = [(b, a) for a, b in steps]
    packed = pack_call(q_short, k_short, v_short, grad_out)
    packed, k_sent, v_sent, q_sent, g_sent = lax.optimization_barrier(
        (packed, k_local, v_local, q_local, grad_out))
    mine = lax.all_to_all(packed, ("c", "z"), split_axis=0, concat_axis=0, tiled=True)
    mine = mine.reshape(-1, 4 * HD)
    halo = jnp.stack([k_sent, v_sent])
    halo_up = jnp.stack([q_sent, g_sent])
    edge = jnp.where(is_first, halo_up, halo)
    halo, halo_up, edge, mine = lax.optimization_barrier((halo, halo_up, edge, mine))
    prev = lax.ppermute(halo, axes, down)
    following = lax.ppermute(halo_up, axes, up)

    chip_rows = mine.shape[0]
    spread = jnp.broadcast_to(mine[None, :, LANES:], (chips, chip_rows, LANES))
    kv = lax.all_to_all(spread, ("x", "y"), split_axis=0, concat_axis=0, tiled=True)
    kv = kv.reshape(-1, LANES)
    cross = lax.ppermute(edge, axes, both_ways)
    od, dkv = short_call(chip, mine, kv, spread)
    dkv, prev, following, cross = lax.optimization_barrier((dkv, prev, following, cross))
    parts = lax.all_to_all(dkv, ("x", "y"), split_axis=0, concat_axis=0, tiled=True)
    prev, od = lax.optimization_barrier((prev, od))
    weights, dscore, stats = weights_call(
        place, q_local, k_local, v_local, grad_out, prev, cross)
    stats = lax.ppermute(stats, axes, all_up)
    local_out, local_dq, own_k, own_v = local_call(
        place, q_local, k_local, v_local, grad_out, prev, cross, weights, dscore)
    local_dk, local_dv, token = late_call(
        place, k_local, v_local, following, cross, stats, own_k, own_v)

    keep, give = reduce_call(core, token, parts, od)
    got = lax.ppermute(give, "c", [(0, 1), (1, 0)])
    short_out, short_dq, short_dk, short_dv = join_call(core, keep, got)
    return (local_out, local_dq, local_dk, local_dv, short_out, short_dq, short_dk, short_dv)


def solution(mesh):
    nx, ny, nc, nz = 4, 4, 2, 8
    sizes = (nx, ny, nc, nz)
    fine = Mesh(mesh.devices.reshape(sizes), ("x", "y", "c", "z"))
    rows = P(("x", "y", "c", "z"), None)
    heads = P(("x", "y", "c"), "z")

    def body(*args):
        return on_device(sizes, *args)

    return jax.shard_map(
        body,
        mesh=fine,
        in_specs=(rows,) * 7,
        out_specs=(rows,) * 4 + (heads,) * 4,
        check_vma=False,
    )
```
